32 devices in a mesh: groups: 2 (over y), gx: 4 (over z), gy: 2 (over x), gz: 2 (over core).
Axes of the slice: x: 2, y: 2, z: 4, core: 2. Of those that a mesh axis runs over, the one named last changes fastest.
Arguments:
- fields: float32 [128, 8, 512], P(('groups', 'gx', 'gy', 'gz')), parts along dimension 0, may hold values from -6 to 6
- courants: float32 [128, 3, 512], P(('groups', 'gx', 'gy', 'gz')), parts along dimension 0, may hold values from -0.3 to 0.3, as said below
- bin_moments: bfloat16 [192, 264, 512], P(('groups', 'gx', 'gy', 'gz')), parts along dimension 0, may hold values from -6 to 6
- block_costs: int32 [128], P('groups'), parts along dimension 0, may hold values from 0 to 2, as said below
- block_owner: int32 [128], P('groups'), parts along dimension 0, may hold values from 0 to 3, as said below
- collision: bfloat16 [66, 4356], replicated, may hold values from -0.029907227 to 0.029907227
Outputs:
- fields_out: float32 [128, 8, 512], P(('groups', 'gx', 'gy', 'gz')), parts along dimension 0
- bins_out: bfloat16 [192, 264, 512], P(('groups', 'gx', 'gy', 'gz')), parts along dimension 0
The draws below stay inside these ranges and needn't reach their ends.
There are 2 independent parts, one for each index of `groups`. The reference program is written for one: setup_inputs(seed, part) draws one part's arguments, and reference() takes and returns one part's arrays. A program takes and returns all parts, laid end to end along the dimension named above; an argument that names none is the same for every part. Nothing has to cross between parts.
Inputs may be any that keep to these rules, and one draw needn't show every extreme that they name: `block_owner`: in every column the blocks of each device of gx form one run of consecutive positions, the runs in the order of the devices; each device holds 2 to 6 blocks of a column, and some device holds 6. `block_costs`: the blocks that one device holds in one column need 4 substeps together. `courants`: the first component lies between 0.05 and 0.3.
All inputs are finite; a program needn't handle non-finite values.
Results may differ from the reference program's by a relative error of at most 0.0058.
Values may be sent and summed in bfloat16 or wider, within the bound.
A program may use at most 64 MiB of HBM per device.

```python
import math
from functools import partial
import jax
import jax.numpy as jnp
from jax import lax

NBIN = 66
NMOM = 4
NFIELD = 8
BX = 8
BY = 8
BZ = 8
ITERS = 2
CAP = 6
NX = 64
NY = 32
NZ = 16
CELLS = 512
BLOCKS = 64
SLOTS = 96
N_GX = 4
N_GY = 2
N_GZ = 2


def column_plan(key):
    columns = N_GY * N_GZ
    places = 4 * N_GX
    shift_pattern = jnp.array([2, -2, 1, -1], jnp.int32)[jnp.arange(N_GX) % 4]
    column_keys = jax.random.split(jax.random.fold_in(key, 11), columns)
    shifts = jax.vmap(lambda column_key: jax.random.permutation(column_key, shift_pattern))(column_keys)
    counts = 4 + shifts
    run_ends = jnp.cumsum(counts, axis=1)
    positions = jnp.arange(places, dtype=jnp.int32)
    owners = jnp.sum((run_ends[:, None, :] <= positions[None, :, None]).astype(jnp.int32), axis=2)
    count_of = jnp.take_along_axis(counts, owners, axis=1)
    scores = jax.random.randint(jax.random.fold_in(key, 12), (columns, places), 0, 1 << 20) * 64 + positions[None, :]
    same_owner = owners[:, :, None] == owners[:, None, :]
    order_rank = jnp.sum((same_owner & (scores[:, None, :] < scores[:, :, None])).astype(jnp.int32), axis=2)
    cost_table = jnp.where(count_of == 2, 2, jnp.where(count_of == 3, jnp.where(order_rank == 0, 2, 1), jnp.where(order_rank < 4, 1, 0)))
    half_rows = N_GX // 2
    owner_tiles = jnp.roll(owners.reshape(columns, N_GX, 4), -half_rows, axis=1)
    cost_tiles = jnp.roll(cost_table.reshape(columns, N_GX, 4), -half_rows, axis=1)
    owner_blocks = owner_tiles.transpose(1, 0, 2).reshape(-1)
    cost_blocks = cost_tiles.transpose(1, 0, 2).reshape(-1)
    return (owner_blocks.astype(jnp.int32), cost_blocks.astype(jnp.int32))


def draw_block_owner(key, part):
    owner_blocks, cost_blocks = column_plan(key)
    return owner_blocks


def draw_block_costs(key, part):
    owner_blocks, cost_blocks = column_plan(key)
    return cost_blocks


def draw_courants(key, part):
    key = jax.random.fold_in(key, 5)
    along = jax.random.uniform(jax.random.fold_in(key, 1), (BLOCKS, 1, CELLS), jnp.float32)
    across = jax.random.uniform(jax.random.fold_in(key, 2), (BLOCKS, 2, CELLS), jnp.float32, -1.0, 1.0)
    along = 0.05 + 0.25 * along
    across = 0.3 * across
    return jnp.concatenate([along, across], axis=1)


def block_scale(rng, shape, cuts, smallest, top_value):
    def one(dim, blocks):
        heights = jax.random.uniform(jax.random.fold_in(jax.random.fold_in(rng, 6), dim), (blocks,), jnp.float32, smallest / len(cuts), top_value / len(cuts))
        return jnp.repeat(jnp.exp(heights), shape[dim] // blocks).reshape((-1,) + (1,) * (len(shape) - dim - 1))

    loudness = one(*cuts[0])
    for cut in cuts[1:]:
        loudness = loudness * one(*cut)
    return loudness


def centred(rng, extent, spread, reach, cuts=(), kind=jnp.bfloat16):
    entries = jax.random.normal(rng, extent, jnp.float32) * spread
    if len(cuts) > 0:
        entries = block_scale(rng, extent, cuts, -0.22, 0.18) * entries
    return jnp.clip(entries, min=-reach, max=reach).astype(kind)


def setup_inputs(seed: int = 0, part: int = 0) -> dict:
    streams_of = jax.random.split(jax.random.key(seed), 7)
    part_splits = jax.random.split(jax.random.fold_in(streams_of[6], part), 7)
    fields = centred(part_splits[0], (BLOCKS, NFIELD, CELLS), 1.0, 6.0, ((0, 16),), jnp.float32)
    courants = draw_courants(jax.random.fold_in(jax.random.fold_in(streams_of[6], part), 71), part)
    bin_moments = centred(part_splits[2], (SLOTS, NMOM * NBIN, CELLS), 1.0, 6.0, ((0, 16),))
    block_costs = draw_block_costs(jax.random.fold_in(jax.random.fold_in(streams_of[6], part), 71), part)
    block_owner = draw_block_owner(jax.random.fold_in(jax.random.fold_in(streams_of[6], part), 71), part)
    collision = centred(streams_of[5], (NBIN, NBIN * NBIN), 0.005, 0.029907227)
    return dict(fields=fields, courants=courants, bin_moments=bin_moments, block_costs=block_costs, block_owner=block_owner, collision=collision)


LATENT = 2.5
SAT_SCALE = 0.5
SAT_SLOPE = 0.2
GROWTH_RATE = 0.02
SOLUTE_WEIGHT = 0.5


def upwind(padded, courant):
    centre = padded[:, 1:-1, 1:-1, 1:-1]
    sides = ((padded[:, :-2, 1:-1, 1:-1], padded[:, 2:, 1:-1, 1:-1]),
             (padded[:, 1:-1, :-2, 1:-1], padded[:, 1:-1, 2:, 1:-1]),
             (padded[:, 1:-1, 1:-1, :-2], padded[:, 1:-1, 1:-1, 2:]))
    result = centre
    for direction in range(3):
        lower_side, upper_side = sides[direction]
        component = courant[direction]
        result = result - jnp.maximum(component, 0.0) * (centre - lower_side)
        result = result - jnp.minimum(component, 0.0) * (upper_side - centre)
    return result


def to_grid(blocks):
    width = blocks.shape[1]
    shaped = blocks.reshape(N_GX, N_GY, N_GZ, 2, 2, width, BX, BY, BZ)
    return shaped.transpose(5, 0, 3, 6, 1, 4, 7, 2, 8).reshape(width, NX, NY, NZ)


def to_blocks(field_grid):
    width = field_grid.shape[0]
    shaped = field_grid.reshape(width, N_GX, 2, BX, N_GY, 2, BY, N_GZ, BZ)
    return shaped.transpose(1, 4, 7, 2, 5, 0, 3, 6, 8).reshape(BLOCKS, width, CELLS)


def process(collision, bin_mass, member):
    block_state, inflow, payload, substeps = member
    nbin = collision.shape[0]
    feature_count, block_cells = block_state.shape
    layer_cells = inflow.shape[1]
    moments = block_state.astype(jnp.float32).reshape(feature_count, block_cells // layer_cells, layer_cells)
    courant = payload[0].reshape(block_cells // layer_cells, layer_cells)
    shifted = jnp.concatenate([inflow.astype(jnp.float32)[:, None, :], moments[:, :-1, :]], axis=1)
    moments = (moments - courant * (moments - shifted)).reshape(feature_count, block_cells)
    number = moments[:nbin]
    mass = moments[nbin:2 * nbin]
    higher = moments[2 * nbin:]

    def collide(counter, carried):
        count_rows, mass_rows = carried
        products = (count_rows[:, None, :] * count_rows[None, :, :]).reshape(nbin * nbin, block_cells).astype(jnp.bfloat16)
        change = jnp.dot(collision, products, preferred_element_type=jnp.float32)
        return count_rows + change, mass_rows + bin_mass[:, None] * change

    number, mass = lax.fori_loop(0, substeps, collide, (number, mass))
    excess = payload[1] - SAT_SCALE * jnp.exp(SAT_SLOPE * payload[2])
    growth = GROWTH_RATE * excess[None, :] * (higher[nbin:] + SOLUTE_WEIGHT * higher[:nbin])
    mass = mass + growth
    joined = jnp.concatenate([number, mass, higher], axis=0)
    return joined.astype(jnp.bfloat16), jnp.sum(growth, axis=0)


def slot_plan(block_owner):
    columns = N_GY * N_GZ
    places = 4 * N_GX
    positions = jnp.arange(places, dtype=jnp.int32)
    column_range = jnp.arange(columns, dtype=jnp.int32)
    tile_row = (positions // 4 + N_GX // 2) % N_GX
    block_ids = (tile_row[None, :] * columns + column_range[:, None]) * 4 + positions[None, :] % 4
    owners = block_owner[block_ids]
    device_range = jnp.arange(N_GX, dtype=jnp.int32)
    counts = jnp.sum((owners[:, :, None] == device_range[None, None, :]).astype(jnp.int32), axis=1)
    starts = jnp.cumsum(counts, axis=1) - counts
    ranks = positions[None, :] - jnp.take_along_axis(starts, owners, axis=1)
    slot_table = (owners * columns + column_range[:, None]) * CAP + ranks
    slot_of_block = jnp.zeros((BLOCKS,), jnp.int32).at[block_ids.reshape(-1)].set(slot_table.reshape(-1))
    slot_range = jnp.arange(SLOTS, dtype=jnp.int32)
    device = slot_range // CAP
    within = slot_range % CAP
    slot_owner = device // columns
    column = device % columns
    slot_start = starts[column, slot_owner]
    slot_count = counts[column, slot_owner]
    slot_place = slot_start + within
    slot_valid = within < slot_count
    clipped = jnp.minimum(slot_place, places - 1)
    block_of_slot = block_ids[column, clipped]
    west_valid = slot_valid & (slot_place >= 2)
    west_slot = slot_of_block[block_ids[column, jnp.clip(slot_place - 2, 0, places - 1)]]
    return slot_of_block, block_of_slot, slot_valid, west_valid, west_slot


def reference(fields, courants, bin_moments, block_costs, block_owner, collision):
    slot_of_block, block_of_slot, slot_valid, west_valid, west_slot = slot_plan(block_owner)
    bin_mass = jnp.exp(jnp.arange(NBIN).astype(jnp.float32) * (math.log(8.0) / (NBIN - 1)))
    courant_grid = to_grid(courants)
    slot_cost = jnp.where(slot_valid, block_costs[block_of_slot], 0).astype(jnp.int32)
    live_mask = slot_valid.astype(jnp.float32)
    face_offset = (BX - 1) * BY * BZ
    blocks = fields
    moment_state = bin_moments
    for iteration in range(ITERS):
        padded = jnp.pad(to_grid(blocks), ((0, 0), (1, 1), (1, 1), (1, 1)))
        blocks = to_blocks(upwind(padded, courant_grid))
        payload = jnp.concatenate([courants[:, 0:1], blocks[:, 1:2], blocks[:, 0:1]], axis=1)
        slot_load = payload[block_of_slot] * live_mask[:, None, None]
        inflows = moment_state[:, :, face_offset:][west_slot]
        inflows = jnp.where(west_valid[:, None, None], inflows, jnp.zeros_like(inflows))
        updated, condensate = lax.map(partial(process, collision, bin_mass),
                                      (moment_state, inflows, slot_load, slot_cost))
        moment_state = jnp.where(slot_valid[:, None, None], updated, jnp.zeros_like(updated))
        condensate = condensate * live_mask[:, None]
        gained = condensate[slot_of_block]
        blocks = jnp.concatenate([blocks[:, 0:1] + LATENT * gained[:, None], blocks[:, 1:2] - gained[:, None], blocks[:, 2:]], axis=1)
    return blocks, moment_state
```

```python
import functools
import math

import jax
import jax.numpy as jnp
from jax import lax
from jax.experimental import pallas as pl
from jax.experimental.pallas import tpu as pltpu
from jax.sharding import PartitionSpec as P

ITERS = 2
SUBSTEPS = 4
LATENT = 2.5
SAT_SCALE = 0.5
SAT_SLOPE = 0.2
GROWTH_RATE = 0.02
SOLUTE_WEIGHT = 0.5
LANES = 128
MESH = pl.DeviceIdType.MESH


def up(value, step):
    return -(-value // step) * step


def pair_plan(nbin):
    padded = up(nbin, 8)
    plan, row = [], 0
    for i in range(nbin):
        low = 8 * (i // 8)
        plan.append((i, low, padded - low, row))
        row += padded - low
    return plan, row


def fold_kernel(nbin, c_ref, w_ref, by_pair, folded):
    plan, rows = pair_plan(nbin)
    for start in range(0, c_ref.shape[1], LANES):
        chunk = c_ref[:, start : start + LANES].astype(jnp.float32)
        by_pair[start : start + LANES, :] = chunk.T
    for i, low, length, row in plan:
        partner = low + lax.broadcasted_iota(jnp.int32, (length, LANES), 0)
        direct = by_pair[pl.ds(nbin * i + low, length), :]
        swapped = by_pair[pl.ds(nbin * low + i, length, stride=nbin), :]
        both = jnp.where(partner > i, direct + swapped, direct)
        keep = (partner >= i) & (partner < nbin)
        folded[row : row + length, :] = jnp.where(keep, both, 0.0)
    folded[rows:, :] = jnp.zeros((folded.shape[0] - rows, LANES), jnp.float32)
    for start in range(0, folded.shape[0], LANES):
        chunk = folded[start : start + LANES, :].T
        w_ref[:, start : start + LANES] = chunk[: w_ref.shape[0]].astype(w_ref.dtype)


def fold(collision):
    nbin, pairs = collision.shape
    plan, rows = pair_plan(nbin)
    depth = up(rows, LANES)
    reach = up(max(pairs, nbin * (up(nbin, 8) - 1) + nbin), LANES)
    padded = jnp.pad(collision, ((0, LANES - nbin), (0, up(pairs, LANES) - pairs)))
    return pl.pallas_call(
        functools.partial(fold_kernel, nbin),
        out_shape=jax.ShapeDtypeStruct((up(nbin, 16), depth), jnp.bfloat16),
        in_specs=[pl.BlockSpec(memory_space=pltpu.VMEM)],
        out_specs=pl.BlockSpec(memory_space=pltpu.VMEM),
        scratch_shapes=[
            pltpu.VMEM((reach, LANES), jnp.float32),
            pltpu.VMEM((depth, LANES), jnp.float32),
        ],
        compiler_params=pltpu.CompilerParams(vmem_limit_bytes=32 * 1024 * 1024),
    )(padded)


def coupled_kernel(
    sizes, nbin,
    owner_ref, cost_ref, fields_ref, courants_ref, bins_ref, w_ref,
    fields_out, bins_out,
    owner_at, rank_at, cost_from, result_of,
    fields_mid, load_mine, load_all, excess_mine, excess_first, excess_second,
    x_low, x_high, y_low, y_high, z_low, z_high,
    face_mine, face_in, sums,
    bins_mid, moved, state, number, products,
    load_send, load_recv, excess_send, excess_recv, halo_send, halo_recv, face_send, face_recv,
):
    gx, gy, gz = sizes["gx"], sizes["gy"], sizes["gz"]
    x, y, z = lax.axis_index("gx"), lax.axis_index("gy"), lax.axis_index("gz")
    half = gx // 2
    places = 4 * gx
    cap = bins_ref.shape[0]
    cells = fields_ref.shape[2]
    columns = gy * gz
    column = y * gz + z
    last = cells - LANES
    f32 = jnp.float32
    padded = up(nbin, 8)
    excess_all = (excess_first, excess_second)

    barrier = pltpu.get_barrier_semaphore()
    for k in range(1, gx):
        pl.semaphore_signal(barrier, inc=1, device_id={"gx": lax.rem(x + k, gx)}, device_id_type=MESH)
    for name, index, count in (("gy", y, gy), ("gz", z, gz)):
        @pl.when(index > 0)
        def _():
            pl.semaphore_signal(barrier, inc=1, device_id={name: index - 1}, device_id_type=MESH)

        @pl.when(index < count - 1)
        def _():
            pl.semaphore_signal(barrier, inc=1, device_id={name: index + 1}, device_id_type=MESH)

    start = jnp.int32(0)
    count = jnp.int32(0)
    before = jnp.int32(-1)
    rank = jnp.int32(0)
    for p in range(places):
        block = (((p // 4 + half) % gx) * columns + column) * 4 + p % 4
        owner = owner_ref[block]
        rank = jnp.where(owner == before, rank + 1, 0)
        before = owner
        owner_at[p] = owner
        rank_at[p] = jnp.minimum(rank, cap - 1)
        start = start + jnp.where(owner < x, 1, 0)
        count = count + jnp.where(owner == x, 1, 0)
    first_row, valid = [], []
    ends = []
    total = jnp.int32(0)
    starts = []
    for s in range(cap):
        place = jnp.minimum(start + s, places - 1)
        tile = lax.rem(place // 4 + half, gx)
        block = (tile * columns + column) * 4 + lax.rem(place, 4)
        occupied = s < count
        valid.append(occupied)
        first_row.append((tile, lax.rem(place, 4)))
        steps = jnp.where(occupied, cost_ref[block], 0)
        starts.append(total)
        total = total + steps
        ends.append(total)
        result_of[s] = jnp.where(steps == 0, s, cap + jnp.clip(total - 1, 0, SUBSTEPS - 1))
    for t in range(SUBSTEPS):
        slot = jnp.int32(0)
        fresh = jnp.int32(0)
        for s in range(cap):
            slot = slot + jnp.where(ends[s] <= t, 1, 0)
            fresh = fresh + jnp.where((starts[s] == t) & (ends[s] > t), 1, 0)
        cost_from[t] = jnp.where(fresh > 0, jnp.minimum(slot, cap - 1), cap + t - 1)

    feature = lax.broadcasted_iota(jnp.int32, (8, bins_ref.shape[1]), 1)
    weights = jnp.where(
        feature >= 3 * nbin, 1.0, jnp.where(feature >= 2 * nbin, SOLUTE_WEIGHT, 0.0)
    ).astype(jnp.bfloat16)
    load_mine[...] = jnp.zeros(load_mine.shape, f32)
    for s in range(cap):
        summed = jnp.dot(weights, bins_ref[s], preferred_element_type=f32)
        load_mine[s : s + 1, :] = summed[0:1]
    for b in range(4):
        load_mine[8 + b : 9 + b, :] = courants_ref[b, 0:1, :]
    load_all[x] = load_mine[...]
    excess_mine[...] = jnp.zeros(excess_mine.shape, f32)

    near = lax.broadcasted_iota(jnp.int32, (1, LANES), 1) < LANES // 2

    def pack_face(ref, it):
        held = jnp.clip(count, 2, cap)
        upper = ref[held - 2, :, last:].astype(f32)
        lower = ref[held - 1, :, last:].astype(f32)
        packed = jnp.where(near, pltpu.roll(upper, LANES // 2, 1), lower)
        face_mine[it] = packed.astype(jnp.bfloat16)

    pack_face(bins_ref, 0)

    def copy(src, dst, send, recv, where):
        return pltpu.make_async_remote_copy(
            src_ref=src, dst_ref=dst, send_sem=send, recv_sem=recv,
            device_id=where, device_id_type=MESH,
        )

    def load_copies():
        return [
            copy(load_mine, load_all.at[x], load_send.at[k - 1], load_recv.at[k - 1],
                 {"gx": lax.rem(x + k, gx)})
            for k in range(1, gx)
        ]

    def excess_copies(it):
        return [
            copy(excess_mine.at[it], excess_all[it].at[x], excess_send.at[it, k - 1],
                 excess_recv.at[it, k - 1], {"gx": lax.rem(x + k, gx)})
            for k in range(1, gx)
        ]

    def halo_copies(src, it):
        out = []
        n = [0]

        def add(has_to, has_from, source, target, where):
            out.append((has_to, has_from, copy(
                source, target, halo_send.at[it, n[0]], halo_recv.at[it, n[0]], where)))
            n[0] += 1

        xu, xd = {"gx": lax.rem(x + 1, gx)}, {"gx": lax.rem(x + gx - 1, gx)}
        yu, yd = {"gy": lax.rem(y + 1, gy)}, {"gy": lax.rem(y + gy - 1, gy)}
        zu, zd = {"gz": lax.rem(z + 1, gz)}, {"gz": lax.rem(z + gz - 1, gz)}
        add(x < gx - 1, x > 0, src.at[pl.ds(2, 2), :, pl.ds(last, LANES)], x_low.at[it], xu)
        add(x > 0, x < gx - 1, src.at[pl.ds(0, 2), :, pl.ds(0, LANES)], x_high.at[it], xd)
        for a in range(2):
            add(y < gy - 1, y > 0, src.at[2 * a + 1], y_low.at[it, a], yu)
            add(y > 0, y < gy - 1, src.at[2 * a], y_high.at[it, a], yd)
        add(z < gz - 1, z > 0, src, z_low.at[it], zu)
        add(z > 0, z < gz - 1, src, z_high.at[it], zd)
        return out

    def face_copy(it):
        return copy(face_mine.at[it], face_in.at[it], face_send.at[it], face_recv.at[it],
                    {"gx": lax.rem(x + 1, gx)})

    def when_do(condition, action):
        @pl.when(condition)
        def _():
            action()

    for low, index in ((x_low, x), (y_low, y), (z_low, z)):
        def clear(low=low):
            low[...] = jnp.zeros(low.shape, f32)
        when_do(index == 0, clear)
    for high, index, size in ((x_high, x, gx), (y_high, y, gy), (z_high, z, gz)):
        def clear(high=high):
            high[...] = jnp.zeros(high.shape, f32)
        when_do(index == size - 1, clear)

    def clear_face():
        face_in[...] = jnp.zeros(face_in.shape, jnp.bfloat16)
    when_do(x == 0, clear_face)

    one = lambda flag: jnp.where(flag, 1, 0)
    pl.semaphore_wait(
        barrier, gx - 1 + one(y > 0) + one(y < gy - 1) + one(z > 0) + one(z < gz - 1)
    )

    halos = [halo_copies(fields_ref, 0), halo_copies(fields_mid, 1)]
    loads = load_copies()
    excesses = [excess_copies(it) for it in range(ITERS)]
    faces = [face_copy(it) for it in range(ITERS)]
    for has_to, has_from, message in halos[0]:
        when_do(has_to, message.start)
    for message in loads:
        message.start()
    when_do(x < gx - 1, faces[0].start)

    for message in loads:
        message.wait_recv()
    base = 4 * lax.rem(x + half, gx)
    sums[...] = jnp.zeros(sums.shape, f32)
    for q in range(6):
        place = jnp.maximum(base - 2 + q, 0)
        row = load_all[owner_at[place], pl.ds(rank_at[place], 1), :]
        if q < 2:
            row = jnp.where(base > 0, row, 0.0)
        sums[0, q : q + 1, :] = row
    sums[1, 0:2, :] = load_all[lax.rem(x + gx - 1, gx), 10:12, :]
    sums[1, 2:6, :] = load_mine[8:12, :]
    along = sums[1]
    cell = lax.broadcasted_iota(jnp.int32, (1, cells), 1)
    layer = LANES // 2

    def sum_transport(value):
        earlier = pltpu.roll(value, 2, 0)
        shifted = jnp.where(cell < layer, pltpu.roll(earlier, layer, 1), pltpu.roll(value, layer, 1))
        return value - along * (value - shifted)

    bin_sums = [sum_transport(sums[0])]
    bin_sums.append(sum_transport(bin_sums[0]))
    yc = lax.rem(cell // 8, 8)
    zc = lax.rem(cell, 8)
    kind = lax.broadcasted_iota(jnp.int32, (8, 1), 0)
    share = jnp.where(kind == 0, LATENT, jnp.where(kind == 1, -1.0, 0.0))

    def dynamics(src, dst, it):
        for has_to, has_from, message in halos[it]:
            when_do(has_from, message.wait_recv)
        for b in range(4):
            a, c = b // 2, b % 2
            g = src[b]
            west = src[b - 2, :, last:] if a else x_low[it, c]
            east = x_high[it, c] if a else src[b + 2, :, :LANES]
            south = src[b - 1] if c else y_low[it, a]
            north = y_high[it, a] if c else src[b + 1]
            wide = cells + LANES
            sides = (
                (pltpu.roll(jnp.concatenate([west, g], axis=1), layer, 1)[:, LANES:],
                 pltpu.roll(jnp.concatenate([g, east], axis=1), wide - layer, 1)[:, :cells]),
                (jnp.where(yc > 0, pltpu.roll(g, 8, 1), pltpu.roll(south, cells - 56, 1)),
                 jnp.where(yc < 7, pltpu.roll(g, cells - 8, 1), pltpu.roll(north, 56, 1))),
                (jnp.where(zc > 0, pltpu.roll(g, 1, 1), pltpu.roll(z_low[it, b], cells - 7, 1)),
                 jnp.where(zc < 7, pltpu.roll(g, cells - 1, 1), pltpu.roll(z_high[it, b], 7, 1))),
            )
            result = g
            for direction in range(3):
                low, high = sides[direction]
                component = courants_ref[b, direction : direction + 1, :]
                result = result - jnp.maximum(component, 0.0) * (g - low)
                result = result - jnp.minimum(component, 0.0) * (high - g)
            excess = result[1:2] - SAT_SCALE * jnp.exp(SAT_SLOPE * result[0:1])
            excess_mine[it, b : b + 1, :] = excess
            gained = GROWTH_RATE * excess * bin_sums[it][2 + b : 3 + b]
            dst[b] = result + share * gained
        excess_all[it][x] = excess_mine[it]
        for message in excesses[it]:
            message.start()

    bin_mass = jnp.exp(
        lax.broadcasted_iota(jnp.int32, (padded, 1), 0).astype(f32) * (math.log(8.0) / (nbin - 1))
    )
    plan, rows = pair_plan(nbin)

    def transport(src, it):
        face = face_in[it].astype(f32)
        for s in range(cap):
            tile, row = first_row[s]
            courant = load_all[tile, pl.ds(8 + row, 1), :]
            if s == 0:
                left = face
            elif s == 1:
                left = pltpu.roll(face, layer, 1)
            else:
                left = pltpu.roll(src[s - 2, :, last:].astype(f32), layer, 1)
            for lane in range(0, cells, LANES):
                u = src[s, :, lane : lane + LANES].astype(f32)
                turned = pltpu.roll(u, layer, 1)
                shifted = jnp.where(near, left, turned)
                left = turned
                moved[s, :, lane : lane + LANES] = u - courant[:, lane : lane + LANES] * (u - shifted)
            state[s, :padded, :] = moved[s, :padded, :]
            state[s, padded:, :] = moved[s, nbin : nbin + padded, :]

    def collide(t, carried):
        source = cost_from[t]
        number[...] = state[source, :padded, :]
        for m in range(0, nbin, 2):
            i, low, length, row = plan[m]
            partners = number[low:, :]
            pair = jnp.concatenate(
                [number[i : i + 1, :] * partners, number[i + 1 : i + 2, :] * partners], axis=0
            )
            products[row : row + 2 * length, :] = pair.astype(jnp.bfloat16)
        change = jnp.dot(w_ref[...], products[...], preferred_element_type=f32)[:padded]
        state[cap + t, :padded, :] = number[...] + change
        state[cap + t, padded:, :] = state[source, padded:, :] + bin_mass * change
        return carried

    def finish(dst, it):
        for s in range(cap):
            tile, row = first_row[s]
            excess = excess_all[it][tile, pl.ds(row, 1), :]
            final = result_of[s]
            growth = (GROWTH_RATE * excess) * (
                moved[s, 3 * nbin :, :] + SOLUTE_WEIGHT * moved[s, 2 * nbin : 3 * nbin, :]
            )
            moved[s, :nbin, :] = state[final, :nbin, :]
            moved[s, nbin : 2 * nbin, :] = state[final, padded : padded + nbin, :] + growth
            value = moved[s]
            if it == ITERS - 1:
                value = jnp.where(valid[s], value, 0.0)
            dst[s] = value.astype(jnp.bfloat16)

    products[rows:, :] = jnp.zeros((products.shape[0] - rows, cells), jnp.bfloat16)

    dynamics(fields_ref, fields_mid, 0)
    for has_to, has_from, message in halos[1]:
        when_do(has_to, message.start)
    when_do(x > 0, faces[0].wait_recv)
    transport(bins_ref, 0)
    lax.fori_loop(0, SUBSTEPS, collide, 0)
    for message in excesses[0]:
        message.wait_recv()
    finish(bins_mid, 0)
    pack_face(bins_mid, 1)
    when_do(x < gx - 1, faces[1].start)
    dynamics(fields_mid, fields_out, 1)
    when_do(x > 0, faces[1].wait_recv)
    transport(bins_mid, 1)
    lax.fori_loop(0, SUBSTEPS, collide, 0)
    for message in excesses[1]:
        message.wait_recv()
    finish(bins_out, 1)

    for it in range(ITERS):
        for has_to, has_from, message in halos[it]:
            when_do(has_to, message.wait_send)
        for message in excesses[it]:
            message.wait_send()
        when_do(x < gx - 1, faces[it].wait_send)
    for message in loads:
        message.wait_send()


def on_device(sizes, fields, courants, bin_moments, block_costs, block_owner, collision):
    nbin = collision.shape[0]
    folded = fold(collision)
    gx = sizes["gx"]
    cap, features, cells = bin_moments.shape
    width = fields.shape[1]
    places = 4 * gx
    padded = up(nbin, 8)
    vmem = pl.BlockSpec(memory_space=pltpu.VMEM)
    smem = pl.BlockSpec(memory_space=pltpu.SMEM)
    f32, bf16 = jnp.float32, jnp.bfloat16
    dma = pltpu.SemaphoreType.DMA
    return pl.pallas_call(
        functools.partial(coupled_kernel, sizes, nbin),
        out_shape=(
            jax.ShapeDtypeStruct(fields.shape, f32),
            jax.ShapeDtypeStruct(bin_moments.shape, bf16),
        ),
        in_specs=[smem, smem, vmem, vmem, vmem, vmem],
        out_specs=(vmem, vmem),
        scratch_shapes=[
            pltpu.SMEM((places,), jnp.int32),
            pltpu.SMEM((places,), jnp.int32),
            pltpu.SMEM((SUBSTEPS,), jnp.int32),
            pltpu.SMEM((cap,), jnp.int32),
            pltpu.VMEM(fields.shape, f32),
            pltpu.VMEM((16, cells), f32),
            pltpu.VMEM((gx, 16, cells), f32),
            pltpu.VMEM((ITERS, 8, cells), f32),
            pltpu.VMEM((gx, 8, cells), f32),
            pltpu.VMEM((gx, 8, cells), f32),
            pltpu.VMEM((ITERS, 2, width, LANES), f32),
            pltpu.VMEM((ITERS, 2, width, LANES), f32),
            pltpu.VMEM((ITERS, 2, width, cells), f32),
            pltpu.VMEM((ITERS, 2, width, cells), f32),
            pltpu.VMEM((ITERS, 4, width, cells), f32),
            pltpu.VMEM((ITERS, 4, width, cells), f32),
            pltpu.VMEM((ITERS, features, LANES), bf16),
            pltpu.VMEM((ITERS, features, LANES), bf16),
            pltpu.VMEM((2, 8, cells), f32),
            pltpu.VMEM(bin_moments.shape, bf16),
            pltpu.VMEM((cap, features, cells), f32),
            pltpu.VMEM((cap + SUBSTEPS, 2 * padded, cells), f32),
            pltpu.VMEM((padded, cells), f32),
            pltpu.VMEM((folded.shape[1], cells), bf16),
            dma((gx - 1,)),
            dma((gx - 1,)),
            dma((ITERS, gx - 1)),
            dma((ITERS, gx - 1)),
            dma((ITERS, 8)),
            dma((ITERS, 8)),
            dma((ITERS,)),
            dma((ITERS,)),
        ],
        compiler_params=pltpu.CompilerParams(
            collective_id=0, has_side_effects=True, vmem_limit_bytes=48 * 1024 * 1024
        ),
    )(block_owner, block_costs, fields, courants, bin_moments, folded)


def solution(mesh):
    parts = P(("groups", "gx", "gy", "gz"), None, None)
    return jax.shard_map(
        functools.partial(on_device, dict(mesh.shape)),
        mesh=mesh,
        in_specs=(parts, parts, parts, P("groups"), P("groups"), P()),
        out_specs=(parts, parts),
        check_vma=False,
    )
```

```python
import functools
import math

import jax
import jax.numpy as jnp
from jax import lax
from jax.experimental import pallas as pl
from jax.experimental.pallas import tpu as pltpu
from jax.sharding import PartitionSpec as P

ITERS = 2
SUBSTEPS = 4
LATENT = 2.5
SAT_SCALE = 0.5
SAT_SLOPE = 0.2
GROWTH_RATE = 0.02
SOLUTE_WEIGHT = 0.5
LANES = 128
MESH = pl.DeviceIdType.MESH


def up(value, step):
    return -(-value // step) * step


def pair_plan(nbin):
    main = 8 * (nbin // 8)
    plan, extra, row = [], [], 0
    for i in range(main):
        low = 8 * (i // 8)
        plan.append((i, low, row))
        r = i - low
        if r >= 1:
            extra.append((row, i, main))
        if r >= 2:
            extra.append((row + 1, i, main + 1))
        if r == 6 and low == 0:
            extra += [(row + 2, main, main), (row + 3, main, main + 1), (row + 4, main + 1, main + 1)]
        if r == 7:
            extra += [(row + 2, low, main), (row + 3, low, main + 1), (row + 4, low + 1, main + 1)]
        row += main - low
    return plan, extra, row, main


def fold(nbin, c_ref, wide, by_pair, folded, w_ref):
    plan, extra, rows, main = pair_plan(nbin)
    pairs = nbin * nbin
    wide[:nbin, :pairs] = c_ref[...].astype(jnp.float32)
    for start in range(0, wide.shape[1], LANES):
        by_pair[start : start + LANES, :] = wide[:, start : start + LANES].T
    for i, low, row in plan:
        length = main - low
        partner = low + lax.broadcasted_iota(jnp.int32, (length, LANES), 0)
        direct = by_pair[pl.ds(nbin * i + low, length), :]
        swapped = by_pair[pl.ds(nbin * low + i, length, stride=nbin), :]
        both = jnp.where(partner > i, direct + swapped, direct)
        folded[row : row + length, :] = jnp.where(partner >= i, both, 0.0)
    for row, i, j in extra:
        value = by_pair[nbin * i + j : nbin * i + j + 1, :]
        if i != j:
            value = value + by_pair[nbin * j + i : nbin * j + i + 1, :]
        folded[row : row + 1, :] = value
    for start in range(0, rows, LANES):
        chunk = folded[start : start + LANES, :].T
        w_ref[:, start : start + LANES] = chunk[: w_ref.shape[0]].astype(w_ref.dtype)


def coupled_kernel(
    sizes, nbin,
    owner_ref, cost_ref, fields_far, courants_far, bins_far, collision_far,
    fields_out, bins_out,
    owner_at, rank_at, cost_from, result_of,
    fields_mid, load_mine, load_all, excess_mine, excess_first, excess_second,
    x_low, x_high, y_low, y_high, z_low, z_high,
    face_mine, face_in, sums,
    bins_mid, moved, state, number, products,
    fields_ref, courants_ref, bins_ref, c_ref, wide, by_pair, folded, w_ref, local_sem,
    load_send, load_recv, excess_send, excess_recv, halo_send, halo_recv, face_send, face_recv,
):
    gx, gy, gz = sizes["gx"], sizes["gy"], sizes["gz"]
    x, y, z = lax.axis_index("gx"), lax.axis_index("gy"), lax.axis_index("gz")
    half = gx // 2
    places = 4 * gx
    cap = bins_ref.shape[0]
    cells = fields_ref.shape[2]
    columns = gy * gz
    column = y * gz + z
    last = cells - LANES
    f32 = jnp.float32
    padded = up(nbin, 8)
    excess_all = (excess_first, excess_second)

    fetches = [
        pltpu.make_async_copy(source, target, local_sem.at[n])
        for n, (source, target) in enumerate((
            (courants_far, courants_ref), (bins_far, bins_ref),
            (fields_far, fields_ref), (collision_far, c_ref)))
    ]
    for fetch in fetches:
        fetch.start()

    barrier = pltpu.get_barrier_semaphore()
    for k in range(1, gx):
        pl.semaphore_signal(barrier, inc=1, device_id={"gx": lax.rem(x + k, gx)}, device_id_type=MESH)
    for name, index, count in (("gy", y, gy), ("gz", z, gz)):
        @pl.when(index > 0)
        def _():
            pl.semaphore_signal(barrier, inc=1, device_id={name: index - 1}, device_id_type=MESH)

        @pl.when(index < count - 1)
        def _():
            pl.semaphore_signal(barrier, inc=1, device_id={name: index + 1}, device_id_type=MESH)

    start = jnp.int32(0)
    count = jnp.int32(0)
    before = jnp.int32(-1)
    rank = jnp.int32(0)
    for p in range(places):
        block = (((p // 4 + half) % gx) * columns + column) * 4 + p % 4
        owner = owner_ref[block]
        rank = jnp.where(owner == before, rank + 1, 0)
        before = owner
        owner_at[p] = owner
        rank_at[p] = jnp.minimum(rank, cap - 1)
        start = start + jnp.where(owner < x, 1, 0)
        count = count + jnp.where(owner == x, 1, 0)
    first_row, valid = [], []
    ends = []
    total = jnp.int32(0)
    starts = []
    for s in range(cap):
        place = jnp.minimum(start + s, places - 1)
        tile = lax.rem(place // 4 + half, gx)
        block = (tile * columns + column) * 4 + lax.rem(place, 4)
        occupied = s < count
        valid.append(occupied)
        first_row.append((tile, lax.rem(place, 4)))
        steps = jnp.where(occupied, cost_ref[block], 0)
        starts.append(total)
        total = total + steps
        ends.append(total)
        result_of[s] = jnp.where(steps == 0, s, cap + jnp.clip(total - 1, 0, SUBSTEPS - 1))
    for t in range(SUBSTEPS):
        slot = jnp.int32(0)
        fresh = jnp.int32(0)
        for s in range(cap):
            slot = slot + jnp.where(ends[s] <= t, 1, 0)
            fresh = fresh + jnp.where((starts[s] == t) & (ends[s] > t), 1, 0)
        cost_from[t] = jnp.where(fresh > 0, jnp.minimum(slot, cap - 1), cap + t - 1)

    feature = lax.broadcasted_iota(jnp.int32, (8, bins_far.shape[1]), 1)
    weights = jnp.where(
        feature >= 3 * nbin, 1.0, jnp.where(feature >= 2 * nbin, SOLUTE_WEIGHT, 0.0)
    ).astype(jnp.bfloat16)
    load_mine[...] = jnp.zeros(load_mine.shape, f32)
    fetches[0].wait()
    fetches[1].wait()
    for s in range(cap):
        summed = jnp.dot(weights, bins_ref[s], preferred_element_type=f32)
        load_mine[s : s + 1, :] = summed[0:1]
    for b in range(4):
        load_mine[8 + b : 9 + b, :] = courants_ref[b, 0:1, :]
    load_all[x] = load_mine[...]
    excess_mine[...] = jnp.zeros(excess_mine.shape, f32)

    near = lax.broadcasted_iota(jnp.int32, (1, LANES), 1) < LANES // 2

    def pack_face(ref, it):
        held = jnp.clip(count, 2, cap)
        upper = ref[held - 2, :, last:].astype(f32)
        lower = ref[held - 1, :, last:].astype(f32)
        packed = jnp.where(near, pltpu.roll(upper, LANES // 2, 1), lower)
        face_mine[it] = packed.astype(jnp.bfloat16)

    pack_face(bins_ref, 0)

    def copy(src, dst, send, recv, where):
        return pltpu.make_async_remote_copy(
            src_ref=src, dst_ref=dst, send_sem=send, recv_sem=recv,
            device_id=where, device_id_type=MESH,
        )

    def load_copies():
        return [
            copy(load_mine, load_all.at[x], load_send.at[k - 1], load_recv.at[k - 1],
                 {"gx": lax.rem(x + k, gx)})
            for k in range(1, gx)
        ]

    def excess_copies(it):
        return [
            copy(excess_mine.at[it], excess_all[it].at[x], excess_send.at[it, k - 1],
                 excess_recv.at[it, k - 1], {"gx": lax.rem(x + k, gx)})
            for k in range(1, gx)
        ]

    def halo_copies(src, it):
        out = []
        n = [0]

        def add(has_to, has_from, source, target, where):
            out.append((has_to, has_from, copy(
                source, target, halo_send.at[it, n[0]], halo_recv.at[it, n[0]], where)))
            n[0] += 1

        xu, xd = {"gx": lax.rem(x + 1, gx)}, {"gx": lax.rem(x + gx - 1, gx)}
        yu, yd = {"gy": lax.rem(y + 1, gy)}, {"gy": lax.rem(y + gy - 1, gy)}
        zu, zd = {"gz": lax.rem(z + 1, gz)}, {"gz": lax.rem(z + gz - 1, gz)}
        add(x < gx - 1, x > 0, src.at[pl.ds(2, 2), :, pl.ds(last, LANES)], x_low.at[it], xu)
        add(x > 0, x < gx - 1, src.at[pl.ds(0, 2), :, pl.ds(0, LANES)], x_high.at[it], xd)
        for a in range(2):
            add(y < gy - 1, y > 0, src.at[2 * a + 1], y_low.at[it, a], yu)
            add(y > 0, y < gy - 1, src.at[2 * a], y_high.at[it, a], yd)
        add(z < gz - 1, z > 0, src, z_low.at[it], zu)
        add(z > 0, z < gz - 1, src, z_high.at[it], zd)
        return out

    def face_copy(it):
        return copy(face_mine.at[it], face_in.at[it], face_send.at[it], face_recv.at[it],
                    {"gx": lax.rem(x + 1, gx)})

    def when_do(condition, action):
        @pl.when(condition)
        def _():
            action()

    for low, index in ((x_low, x), (y_low, y), (z_low, z)):
        def clear(low=low):
            low[...] = jnp.zeros(low.shape, f32)
        when_do(index == 0, clear)
    for high, index, size in ((x_high, x, gx), (y_high, y, gy), (z_high, z, gz)):
        def clear(high=high):
            high[...] = jnp.zeros(high.shape, f32)
        when_do(index == size - 1, clear)

    def clear_face():
        face_in[...] = jnp.zeros(face_in.shape, jnp.bfloat16)
    when_do(x == 0, clear_face)

    one = lambda flag: jnp.where(flag, 1, 0)
    pl.semaphore_wait(
        barrier, gx - 1 + one(y > 0) + one(y < gy - 1) + one(z > 0) + one(z < gz - 1)
    )

    halos = [halo_copies(fields_far, 0), halo_copies(fields_mid, 1)]
    loads = load_copies()
    excesses = [excess_copies(it) for it in range(ITERS)]
    faces = [face_copy(it) for it in range(ITERS)]
    for has_to, has_from, message in halos[0]:
        when_do(has_to, message.start)
    for message in loads:
        message.start()
    when_do(x < gx - 1, faces[0].start)

    fetches[3].wait()
    wide[nbin:, :] = jnp.zeros((LANES - nbin, wide.shape[1]), f32)
    wide[:nbin, wide.shape[1] - LANES :] = jnp.zeros((nbin, LANES), f32)
    fold(nbin, c_ref, wide, by_pair, folded, w_ref)
    fetches[2].wait()

    for message in loads:
        message.wait_recv()
    base = 4 * lax.rem(x + half, gx)
    sums[...] = jnp.zeros(sums.shape, f32)
    for q in range(6):
        place = jnp.maximum(base - 2 + q, 0)
        row = load_all[owner_at[place], pl.ds(rank_at[place], 1), :]
        if q < 2:
            row = jnp.where(base > 0, row, 0.0)
        sums[0, q : q + 1, :] = row
    sums[1, 0:2, :] = load_all[lax.rem(x + gx - 1, gx), 10:12, :]
    sums[1, 2:6, :] = load_mine[8:12, :]
    along = sums[1]
    cell = lax.broadcasted_iota(jnp.int32, (1, cells), 1)
    layer = LANES // 2

    def sum_transport(value):
        earlier = pltpu.roll(value, 2, 0)
        shifted = jnp.where(cell < layer, pltpu.roll(earlier, layer, 1), pltpu.roll(value, layer, 1))
        return value - along * (value - shifted)

    bin_sums = [sum_transport(sums[0])]
    bin_sums.append(sum_transport(bin_sums[0]))
    yc = lax.rem(cell // 8, 8)
    zc = lax.rem(cell, 8)
    kind = lax.broadcasted_iota(jnp.int32, (8, 1), 0)
    share = jnp.where(kind == 0, LATENT, jnp.where(kind == 1, -1.0, 0.0))

    def dynamics(src, dst, it):
        for has_to, has_from, message in halos[it]:
            when_do(has_from, message.wait_recv)
        for b in range(4):
            a, c = b // 2, b % 2
            g = src[b]
            west = src[b - 2, :, last:] if a else x_low[it, c]
            east = x_high[it, c] if a else src[b + 2, :, :LANES]
            south = src[b - 1] if c else y_low[it, a]
            north = y_high[it, a] if c else src[b + 1]
            wide = cells + LANES
            sides = (
                (pltpu.roll(jnp.concatenate([west, g], axis=1), layer, 1)[:, LANES:],
                 pltpu.roll(jnp.concatenate([g, east], axis=1), wide - layer, 1)[:, :cells]),
                (jnp.where(yc > 0, pltpu.roll(g, 8, 1), pltpu.roll(south, cells - 56, 1)),
                 jnp.where(yc < 7, pltpu.roll(g, cells - 8, 1), pltpu.roll(north, 56, 1))),
                (jnp.where(zc > 0, pltpu.roll(g, 1, 1), pltpu.roll(z_low[it, b], cells - 7, 1)),
                 jnp.where(zc < 7, pltpu.roll(g, cells - 1, 1), pltpu.roll(z_high[it, b], 7, 1))),
            )
            result = g
            for direction in range(3):
                low, high = sides[direction]
                component = courants_ref[b, direction : direction + 1, :]
                result = result - jnp.maximum(component, 0.0) * (g - low)
                result = result - jnp.minimum(component, 0.0) * (high - g)
            excess = result[1:2] - SAT_SCALE * jnp.exp(SAT_SLOPE * result[0:1])
            excess_mine[it, b : b + 1, :] = excess
            gained = GROWTH_RATE * excess * bin_sums[it][2 + b : 3 + b]
            dst[b] = result + share * gained
        excess_all[it][x] = excess_mine[it]
        for message in excesses[it]:
            message.start()

    bin_mass = jnp.exp(
        lax.broadcasted_iota(jnp.int32, (padded, 1), 0).astype(f32) * (math.log(8.0) / (nbin - 1))
    )
    plan, extra, rows, main = pair_plan(nbin)
    eighth = lax.broadcasted_iota(jnp.int32, (8, 1), 0)

    def transport(src, it):
        face = face_in[it].astype(f32)
        for s in range(cap):
            tile, row = first_row[s]
            courant = load_all[tile, pl.ds(8 + row, 1), :]
            if s == 0:
                left = face
            elif s == 1:
                left = pltpu.roll(face, layer, 1)
            else:
                left = pltpu.roll(src[s - 2, :, last:].astype(f32), layer, 1)
            for lane in range(0, cells, LANES):
                u = src[s, :, lane : lane + LANES].astype(f32)
                turned = pltpu.roll(u, layer, 1)
                shifted = jnp.where(near, left, turned)
                left = turned
                moved[s, :, lane : lane + LANES] = u - courant[:, lane : lane + LANES] * (u - shifted)
            state[s, :padded, :] = moved[s, :padded, :]
            state[s, padded:, :] = moved[s, nbin : nbin + padded, :]

    def collide(t, carried):
        source = cost_from[t]
        number[...] = state[source, :padded, :]
        above = number[main : main + 1, :]
        top = number[main + 1 : main + 2, :]
        above_first = jnp.where(eighth % 2 == 0, above, top)
        for m in range(0, main, 2):
            pieces = []
            for i, low, row in plan[m : m + 2]:
                r = i - low
                own = number[i : i + 1, :]
                diagonal = number[low : low + 8, :]
                left = own
                if r == 1:
                    diagonal = jnp.where(eighth == 0, above, diagonal)
                elif r >= 2:
                    diagonal = jnp.where(eighth < 2, above_first, diagonal)
                if r == 6 and low == 0:
                    left = jnp.where((eighth == 2) | (eighth == 3), above, own)
                    left = jnp.where(eighth == 4, top, left)
                if r == 7:
                    first, second = number[low : low + 1, :], number[low + 1 : low + 2, :]
                    left = jnp.where((eighth == 2) | (eighth == 3), first, own)
                    left = jnp.where(eighth == 4, second, left)
                if r == 7 or (r == 6 and low == 0):
                    middle = (eighth >= 2) & (eighth < 4)
                    diagonal = jnp.where(middle, above_first, diagonal)
                    diagonal = jnp.where(eighth == 4, top, diagonal)
                pieces.append(left * diagonal)
                if low + 8 < main:
                    pieces.append(own * number[low + 8 : main, :])
            pair = jnp.concatenate(pieces, axis=0)
            row = plan[m][2]
            products[row : row + pair.shape[0], :] = pair.astype(jnp.bfloat16)
        change = jnp.dot(w_ref[...], products[...], preferred_element_type=f32)[:padded]
        state[cap + t, :padded, :] = number[...] + change
        state[cap + t, padded:, :] = state[source, padded:, :] + bin_mass * change
        return carried

    def finish(dst, it):
        for s in range(cap):
            tile, row = first_row[s]
            excess = excess_all[it][tile, pl.ds(row, 1), :]
            final = result_of[s]
            growth = (GROWTH_RATE * excess) * (
                moved[s, 3 * nbin :, :] + SOLUTE_WEIGHT * moved[s, 2 * nbin : 3 * nbin, :]
            )
            moved[s, :nbin, :] = state[final, :nbin, :]
            moved[s, nbin : 2 * nbin, :] = state[final, padded : padded + nbin, :] + growth
            value = moved[s]
            if it == ITERS - 1:
                value = jnp.where(valid[s], value, 0.0)
            dst[s] = value.astype(jnp.bfloat16)

    dynamics(fields_ref, fields_mid, 0)
    for has_to, has_from, message in halos[1]:
        when_do(has_to, message.start)
    when_do(x > 0, faces[0].wait_recv)
    transport(bins_ref, 0)
    lax.fori_loop(0, SUBSTEPS, collide, 0)
    for message in excesses[0]:
        message.wait_recv()
    finish(bins_mid, 0)
    pack_face(bins_mid, 1)
    when_do(x < gx - 1, faces[1].start)
    dynamics(fields_mid, fields_out, 1)
    when_do(x > 0, faces[1].wait_recv)
    transport(bins_mid, 1)
    lax.fori_loop(0, SUBSTEPS, collide, 0)
    for message in excesses[1]:
        message.wait_recv()
    finish(bins_out, 1)

    for it in range(ITERS):
        for has_to, has_from, message in halos[it]:
            when_do(has_to, message.wait_send)
        for message in excesses[it]:
            message.wait_send()
        when_do(x < gx - 1, faces[it].wait_send)
    for message in loads:
        message.wait_send()


def on_device(sizes, fields, courants, bin_moments, block_costs, block_owner, collision):
    nbin = collision.shape[0]
    plan, extra, rows, main = pair_plan(nbin)
    wide = up(nbin * nbin, LANES)
    any_space = pl.BlockSpec(memory_space=pl.ANY)
    gx = sizes["gx"]
    cap, features, cells = bin_moments.shape
    width = fields.shape[1]
    places = 4 * gx
    padded = up(nbin, 8)
    vmem = pl.BlockSpec(memory_space=pltpu.VMEM)
    smem = pl.BlockSpec(memory_space=pltpu.SMEM)
    f32, bf16 = jnp.float32, jnp.bfloat16
    dma = pltpu.SemaphoreType.DMA
    return pl.pallas_call(
        functools.partial(coupled_kernel, sizes, nbin),
        out_shape=(
            jax.ShapeDtypeStruct(fields.shape, f32),
            jax.ShapeDtypeStruct(bin_moments.shape, bf16),
        ),
        in_specs=[smem, smem] + [any_space] * 4,
        out_specs=(vmem, vmem),
        scratch_shapes=[
            pltpu.SMEM((places,), jnp.int32),
            pltpu.SMEM((places,), jnp.int32),
            pltpu.SMEM((SUBSTEPS,), jnp.int32),
            pltpu.SMEM((cap,), jnp.int32),
            pltpu.VMEM(fields.shape, f32),
            pltpu.VMEM((16, cells), f32),
            pltpu.VMEM((gx, 16, cells), f32),
            pltpu.VMEM((ITERS, 8, cells), f32),
            pltpu.VMEM((gx, 8, cells), f32),
            pltpu.VMEM((gx, 8, cells), f32),
            pltpu.VMEM((ITERS, 2, width, LANES), f32),
            pltpu.VMEM((ITERS, 2, width, LANES), f32),
            pltpu.VMEM((ITERS, 2, width, cells), f32),
            pltpu.VMEM((ITERS, 2, width, cells), f32),
            pltpu.VMEM((ITERS, 4, width, cells), f32),
            pltpu.VMEM((ITERS, 4, width, cells), f32),
            pltpu.VMEM((ITERS, features, LANES), bf16),
            pltpu.VMEM((ITERS, features, LANES), bf16),
            pltpu.VMEM((2, 8, cells), f32),
            pltpu.VMEM(bin_moments.shape, bf16),
            pltpu.VMEM((cap, features, cells), f32),
            pltpu.VMEM((cap + SUBSTEPS, 2 * padded, cells), f32),
            pltpu.VMEM((padded, cells), f32),
            pltpu.VMEM((rows, cells), bf16),
            pltpu.VMEM(fields.shape, f32),
            pltpu.VMEM(courants.shape, f32),
            pltpu.VMEM(bin_moments.shape, bf16),
            pltpu.VMEM(collision.shape, bf16),
            pltpu.VMEM((LANES, wide), f32),
            pltpu.VMEM((wide, LANES), f32),
            pltpu.VMEM((rows, LANES), f32),
            pltpu.VMEM((up(nbin, 16), rows), bf16),
            dma((4,)),
            dma((gx - 1,)),
            dma((gx - 1,)),
            dma((ITERS, gx - 1)),
            dma((ITERS, gx - 1)),
            dma((ITERS, 8)),
            dma((ITERS, 8)),
            dma((ITERS,)),
            dma((ITERS,)),
        ],
        compiler_params=pltpu.CompilerParams(
            collective_id=0, has_side_effects=True, vmem_limit_bytes=48 * 1024 * 1024
        ),
    )(block_owner, block_costs, fields, courants, bin_moments, collision)


def solution(mesh):
    parts = P(("groups", "gx", "gy", "gz"), None, None)
    return jax.shard_map(
        functools.partial(on_device, dict(mesh.shape)),
        mesh=mesh,
        in_specs=(parts, parts, parts, P("groups"), P("groups"), P()),
        out_specs=(parts, parts),
        check_vma=False,
    )
```

```python
import functools
import math

import jax
import jax.numpy as jnp
from jax import lax
from jax.experimental import pallas as pl
from jax.experimental.pallas import tpu as pltpu
from jax.sharding import PartitionSpec as P

ITERS = 2
SUBSTEPS = 4
LATENT = 2.5
SAT_SCALE = 0.5
SAT_SLOPE = 0.2
GROWTH_RATE = 0.02
SOLUTE_WEIGHT = 0.5
LANES = 128
MESH = pl.DeviceIdType.MESH


def up(value, step):
    return -(-value // step) * step


def pair_plan(nbin):
    main = 8 * (nbin // 8)
    plan, extra, row = [], [], 0
    for i in range(main):
        low = 8 * (i // 8)
        plan.append((i, low, row))
        r = i - low
        if r >= 1:
            extra.append((row, i, main))
        if r >= 2:
            extra.append((row + 1, i, main + 1))
        if r == 6 and low == 0:
            extra += [(row + 2, main, main), (row + 3, main, main + 1), (row + 4, main + 1, main + 1)]
        if r == 7:
            extra += [(row + 2, low, main), (row + 3, low, main + 1), (row + 4, low + 1, main + 1)]
        row += main - low
    return plan, extra, row, main


def fold(nbin, c_ref, wide, by_pair, folded, w_ref):
    plan, extra, rows, main = pair_plan(nbin)
    pairs = nbin * nbin
    wide[:nbin, :pairs] = c_ref[...].astype(jnp.float32)
    for start in range(0, wide.shape[1], LANES):
        by_pair[start : start + LANES, :] = wide[:, start : start + LANES].T
    for i, low, row in plan:
        length = main - low
        partner = low + lax.broadcasted_iota(jnp.int32, (length, LANES), 0)
        direct = by_pair[pl.ds(nbin * i + low, length), :]
        swapped = by_pair[pl.ds(nbin * low + i, length, stride=nbin), :]
        both = jnp.where(partner > i, direct + swapped, direct)
        folded[row : row + length, :] = jnp.where(partner >= i, both, 0.0)
    for row, i, j in extra:
        value = by_pair[nbin * i + j : nbin * i + j + 1, :]
        if i != j:
            value = value + by_pair[nbin * j + i : nbin * j + i + 1, :]
        folded[row : row + 1, :] = value
    for start in range(0, rows, LANES):
        chunk = folded[start : start + LANES, :].T
        w_ref[:, start : start + LANES] = chunk[: w_ref.shape[0]].astype(w_ref.dtype)


def coupled_kernel(
    sizes, nbin,
    owner_far, cost_far, fields_far, courants_far, bins_far, collision_far,
    fields_out, bins_out,
    owner_ref, cost_ref, owner_at, rank_at, cost_from, result_of,
    fields_mid, load_mine, load_all, excess_mine, excess_first, excess_second,
    x_low, x_high, y_low, y_high, z_low, z_high,
    face_mine, face_in, sums,
    bins_mid, moved, state, number, products,
    fields_ref, courants_ref, bins_ref, c_ref, wide, by_pair, folded, w_ref, local_sem,
    load_send, load_recv, excess_send, excess_recv, halo_send, halo_recv, face_send, face_recv,
):
    gx, gy, gz = sizes["gx"], sizes["gy"], sizes["gz"]
    x, y, z = lax.axis_index("gx"), lax.axis_index("gy"), lax.axis_index("gz")
    half = gx // 2
    places = 4 * gx
    cap = bins_ref.shape[0]
    cells = fields_ref.shape[2]
    columns = gy * gz
    column = y * gz + z
    last = cells - LANES
    f32 = jnp.float32
    padded = up(nbin, 8)
    excess_all = (excess_first, excess_second)

    fetches = [
        pltpu.make_async_copy(source, target, local_sem.at[n])
        for n, (source, target) in enumerate((
            (courants_far, courants_ref), (bins_far, bins_ref),
            (fields_far, fields_ref), (collision_far, c_ref),
            (owner_far, owner_ref), (cost_far, cost_ref)))
    ]
    for n in (4, 5, 0, 1, 3, 2):
        fetches[n].start()

    barrier = pltpu.get_barrier_semaphore()
    for k in range(1, gx):
        pl.semaphore_signal(barrier, inc=1, device_id={"gx": lax.rem(x + k, gx)}, device_id_type=MESH)
    for name, index, count in (("gy", y, gy), ("gz", z, gz)):
        @pl.when(index > 0)
        def _():
            pl.semaphore_signal(barrier, inc=1, device_id={name: index - 1}, device_id_type=MESH)

        @pl.when(index < count - 1)
        def _():
            pl.semaphore_signal(barrier, inc=1, device_id={name: index + 1}, device_id_type=MESH)

    fetches[4].wait()
    fetches[5].wait()
    start = jnp.int32(0)
    count = jnp.int32(0)
    before = jnp.int32(-1)
    rank = jnp.int32(0)
    for p in range(places):
        block = (((p // 4 + half) % gx) * columns + column) * 4 + p % 4
        owner = owner_ref[block]
        rank = jnp.where(owner == before, rank + 1, 0)
        before = owner
        owner_at[p] = owner
        rank_at[p] = jnp.minimum(rank, cap - 1)
        start = start + jnp.where(owner < x, 1, 0)
        count = count + jnp.where(owner == x, 1, 0)
    first_row, valid = [], []
    ends = []
    total = jnp.int32(0)
    starts = []
    for s in range(cap):
        place = jnp.minimum(start + s, places - 1)
        tile = lax.rem(place // 4 + half, gx)
        block = (tile * columns + column) * 4 + lax.rem(place, 4)
        occupied = s < count
        valid.append(occupied)
        first_row.append((tile, lax.rem(place, 4)))
        steps = jnp.where(occupied, cost_ref[block], 0)
        starts.append(total)
        total = total + steps
        ends.append(total)
        result_of[s] = jnp.where(steps == 0, s, cap + jnp.clip(total - 1, 0, SUBSTEPS - 1))
    for t in range(SUBSTEPS):
        slot = jnp.int32(0)
        fresh = jnp.int32(0)
        for s in range(cap):
            slot = slot + jnp.where(ends[s] <= t, 1, 0)
            fresh = fresh + jnp.where((starts[s] == t) & (ends[s] > t), 1, 0)
        cost_from[t] = jnp.where(fresh > 0, jnp.minimum(slot, cap - 1), cap + t - 1)

    feature = lax.broadcasted_iota(jnp.int32, (8, bins_far.shape[1]), 1)
    weights = jnp.where(
        feature >= 3 * nbin, 1.0, jnp.where(feature >= 2 * nbin, SOLUTE_WEIGHT, 0.0)
    ).astype(jnp.bfloat16)
    load_mine[...] = jnp.zeros(load_mine.shape, f32)
    fetches[0].wait()
    fetches[1].wait()
    for s in range(cap):
        summed = jnp.dot(weights, bins_ref[s], preferred_element_type=f32)
        load_mine[s : s + 1, :] = summed[0:1]
    for b in range(4):
        load_mine[8 + b : 9 + b, :] = courants_ref[0, b : b + 1, :]
    load_all[x] = load_mine[...]
    excess_mine[...] = jnp.zeros(excess_mine.shape, f32)

    near = lax.broadcasted_iota(jnp.int32, (1, LANES), 1) < LANES // 2

    def pack_face(ref, it):
        held = jnp.clip(count, 2, cap)
        upper = ref[held - 2, :, last:].astype(f32)
        lower = ref[held - 1, :, last:].astype(f32)
        packed = jnp.where(near, pltpu.roll(upper, LANES // 2, 1), lower)
        face_mine[it] = packed.astype(jnp.bfloat16)

    pack_face(bins_ref, 0)

    def copy(src, dst, send, recv, where):
        return pltpu.make_async_remote_copy(
            src_ref=src, dst_ref=dst, send_sem=send, recv_sem=recv,
            device_id=where, device_id_type=MESH,
        )

    def load_copies():
        return [
            copy(load_mine, load_all.at[x], load_send.at[k - 1], load_recv.at[k - 1],
                 {"gx": lax.rem(x + k, gx)})
            for k in range(1, gx)
        ]

    def excess_copies(it):
        return [
            copy(excess_mine.at[it], excess_all[it].at[x], excess_send.at[it, k - 1],
                 excess_recv.at[it, k - 1], {"gx": lax.rem(x + k, gx)})
            for k in range(1, gx)
        ]

    def halo_copies(src, it):
        out = []
        n = [0]

        def add(has_to, has_from, source, target, where):
            out.append((has_to, has_from, copy(
                source, target, halo_send.at[it, n[0]], halo_recv.at[it, n[0]], where)))
            n[0] += 1

        xu, xd = {"gx": lax.rem(x + 1, gx)}, {"gx": lax.rem(x + gx - 1, gx)}
        yu, yd = {"gy": lax.rem(y + 1, gy)}, {"gy": lax.rem(y + gy - 1, gy)}
        zu, zd = {"gz": lax.rem(z + 1, gz)}, {"gz": lax.rem(z + gz - 1, gz)}
        add(x < gx - 1, x > 0, src.at[pl.ds(2, 2), :, pl.ds(last, LANES)], x_low.at[it], xu)
        add(x > 0, x < gx - 1, src.at[pl.ds(0, 2), :, pl.ds(0, LANES)], x_high.at[it], xd)
        for a in range(2):
            add(y < gy - 1, y > 0, src.at[2 * a + 1], y_low.at[it, a], yu)
            add(y > 0, y < gy - 1, src.at[2 * a], y_high.at[it, a], yd)
        add(z < gz - 1, z > 0, src, z_low.at[it], zu)
        add(z > 0, z < gz - 1, src, z_high.at[it], zd)
        return out

    def face_copy(it):
        return copy(face_mine.at[it], face_in.at[it], face_send.at[it], face_recv.at[it],
                    {"gx": lax.rem(x + 1, gx)})

    def when_do(condition, action):
        @pl.when(condition)
        def _():
            action()

    for low, index in ((x_low, x), (y_low, y), (z_low, z)):
        def clear(low=low):
            low[...] = jnp.zeros(low.shape, f32)
        when_do(index == 0, clear)
    for high, index, size in ((x_high, x, gx), (y_high, y, gy), (z_high, z, gz)):
        def clear(high=high):
            high[...] = jnp.zeros(high.shape, f32)
        when_do(index == size - 1, clear)

    def clear_face():
        face_in[...] = jnp.zeros(face_in.shape, jnp.bfloat16)
    when_do(x == 0, clear_face)

    one = lambda flag: jnp.where(flag, 1, 0)
    pl.semaphore_wait(
        barrier, gx - 1 + one(y > 0) + one(y < gy - 1) + one(z > 0) + one(z < gz - 1)
    )

    halos = [halo_copies(fields_far, 0), halo_copies(fields_mid, 1)]
    loads = load_copies()
    excesses = [excess_copies(it) for it in range(ITERS)]
    faces = [face_copy(it) for it in range(ITERS)]
    for has_to, has_from, message in halos[0]:
        when_do(has_to, message.start)
    for message in loads:
        message.start()
    when_do(x < gx - 1, faces[0].start)

    fetches[3].wait()
    wide[nbin:, :] = jnp.zeros((LANES - nbin, wide.shape[1]), f32)
    wide[:nbin, wide.shape[1] - LANES :] = jnp.zeros((nbin, LANES), f32)
    fold(nbin, c_ref, wide, by_pair, folded, w_ref)
    fetches[2].wait()

    for message in loads:
        message.wait_recv()
    base = 4 * lax.rem(x + half, gx)
    sums[...] = jnp.zeros(sums.shape, f32)
    for q in range(6):
        place = jnp.maximum(base - 2 + q, 0)
        row = load_all[owner_at[place], pl.ds(rank_at[place], 1), :]
        if q < 2:
            row = jnp.where(base > 0, row, 0.0)
        sums[0, q : q + 1, :] = row
    sums[1, 0:2, :] = load_all[lax.rem(x + gx - 1, gx), 10:12, :]
    sums[1, 2:6, :] = load_mine[8:12, :]
    along = sums[1]
    cell = lax.broadcasted_iota(jnp.int32, (1, cells), 1)
    layer = LANES // 2

    def sum_transport(value):
        earlier = pltpu.roll(value, 2, 0)
        shifted = jnp.where(cell < layer, pltpu.roll(earlier, layer, 1), pltpu.roll(value, layer, 1))
        return value - along * (value - shifted)

    bin_sums = [sum_transport(sums[0])]
    bin_sums.append(sum_transport(bin_sums[0]))
    yc = lax.rem(cell // 8, 8)
    zc = lax.rem(cell, 8)
    kind = lax.broadcasted_iota(jnp.int32, (8, 1), 0)
    share = jnp.where(kind == 0, LATENT, jnp.where(kind == 1, -1.0, 0.0))

    def dynamics(src, dst, it):
        for has_to, has_from, message in halos[it]:
            when_do(has_from, message.wait_recv)
        for b in range(4):
            a, c = b // 2, b % 2
            g = src[b]
            west = src[b - 2, :, last:] if a else x_low[it, c]
            east = x_high[it, c] if a else src[b + 2, :, :LANES]
            south = src[b - 1] if c else y_low[it, a]
            north = y_high[it, a] if c else src[b + 1]
            wide = cells + LANES
            sides = (
                (pltpu.roll(jnp.concatenate([west, g], axis=1), layer, 1)[:, LANES:],
                 pltpu.roll(jnp.concatenate([g, east], axis=1), wide - layer, 1)[:, :cells]),
                (jnp.where(yc > 0, pltpu.roll(g, 8, 1), pltpu.roll(south, cells - 56, 1)),
                 jnp.where(yc < 7, pltpu.roll(g, cells - 8, 1), pltpu.roll(north, 56, 1))),
                (jnp.where(zc > 0, pltpu.roll(g, 1, 1), pltpu.roll(z_low[it, b], cells - 7, 1)),
                 jnp.where(zc < 7, pltpu.roll(g, cells - 1, 1), pltpu.roll(z_high[it, b], 7, 1))),
            )
            result = g
            for direction in range(3):
                low, high = sides[direction]
                component = courants_ref[direction, b : b + 1, :]
                result = result - jnp.maximum(component, 0.0) * (g - low)
                result = result - jnp.minimum(component, 0.0) * (high - g)
            excess = result[1:2] - SAT_SCALE * jnp.exp(SAT_SLOPE * result[0:1])
            excess_mine[it, b : b + 1, :] = excess
            gained = GROWTH_RATE * excess * bin_sums[it][2 + b : 3 + b]
            dst[b] = result + share * gained
        excess_all[it][x] = excess_mine[it]
        for message in excesses[it]:
            message.start()

    bin_mass = jnp.exp(
        lax.broadcasted_iota(jnp.int32, (padded, 1), 0).astype(f32) * (math.log(8.0) / (nbin - 1))
    )
    plan, extra, rows, main = pair_plan(nbin)
    eighth = lax.broadcasted_iota(jnp.int32, (8, 1), 0)

    def transport(src, it):
        face = face_in[it].astype(f32)
        for s in range(cap):
            tile, row = first_row[s]
            courant = load_all[tile, pl.ds(8 + row, 1), :]
            if s == 0:
                left = face
            elif s == 1:
                left = pltpu.roll(face, layer, 1)
            else:
                left = pltpu.roll(src[s - 2, :, last:].astype(f32), layer, 1)
            for lane in range(0, cells, LANES):
                u = src[s, :, lane : lane + LANES].astype(f32)
                turned = pltpu.roll(u, layer, 1)
                shifted = jnp.where(near, left, turned)
                left = turned
                moved[s, :, lane : lane + LANES] = u - courant[:, lane : lane + LANES] * (u - shifted)
            state[s, :padded, :] = moved[s, :padded, :]
            state[s, padded:, :] = moved[s, nbin : nbin + padded, :]

    def collide(t, carried):
        source = cost_from[t]
        number[...] = state[source, :padded, :]
        above = number[main : main + 1, :]
        top = number[main + 1 : main + 2, :]
        above_first = jnp.where(eighth % 2 == 0, above, top)
        for m in range(0, main, 2):
            pieces = []
            for i, low, row in plan[m : m + 2]:
                r = i - low
                own = number[i : i + 1, :]
                diagonal = number[low : low + 8, :]
                left = own
                if r == 1:
                    diagonal = jnp.where(eighth == 0, above, diagonal)
                elif r >= 2:
                    diagonal = jnp.where(eighth < 2, above_first, diagonal)
                if r == 6 and low == 0:
                    left = jnp.where((eighth == 2) | (eighth == 3), above, own)
                    left = jnp.where(eighth == 4, top, left)
                if r == 7:
                    first, second = number[low : low + 1, :], number[low + 1 : low + 2, :]
                    left = jnp.where((eighth == 2) | (eighth == 3), first, own)
                    left = jnp.where(eighth == 4, second, left)
                if r == 7 or (r == 6 and low == 0):
                    middle = (eighth >= 2) & (eighth < 4)
                    diagonal = jnp.where(middle, above_first, diagonal)
                    diagonal = jnp.where(eighth == 4, top, diagonal)
                pieces.append(left * diagonal)
                if low + 8 < main:
                    pieces.append(own * number[low + 8 : main, :])
            pair = jnp.concatenate(pieces, axis=0)
            row = plan[m][2]
            products[row : row + pair.shape[0], :] = pair.astype(jnp.bfloat16)
        change = jnp.dot(w_ref[...], products[...], preferred_element_type=f32)[:padded]
        state[cap + t, :padded, :] = number[...] + change
        state[cap + t, padded:, :] = state[source, padded:, :] + bin_mass * change
        return carried

    def finish(dst, it):
        for s in range(cap):
            tile, row = first_row[s]
            excess = excess_all[it][tile, pl.ds(row, 1), :]
            final = result_of[s]
            growth = (GROWTH_RATE * excess) * (
                moved[s, 3 * nbin :, :] + SOLUTE_WEIGHT * moved[s, 2 * nbin : 3 * nbin, :]
            )
            moved[s, :nbin, :] = state[final, :nbin, :]
            moved[s, nbin : 2 * nbin, :] = state[final, padded : padded + nbin, :] + growth
            value = moved[s]
            if it == ITERS - 1:
                value = jnp.where(valid[s], value, 0.0)
            dst[s] = value.astype(jnp.bfloat16)

    dynamics(fields_ref, fields_mid, 0)
    for has_to, has_from, message in halos[1]:
        when_do(has_to, message.start)
    when_do(x > 0, faces[0].wait_recv)
    transport(bins_ref, 0)
    lax.fori_loop(0, SUBSTEPS, collide, 0)
    for message in excesses[0]:
        message.wait_recv()
    finish(bins_mid, 0)
    pack_face(bins_mid, 1)
    when_do(x < gx - 1, faces[1].start)
    dynamics(fields_mid, fields_out, 1)
    when_do(x > 0, faces[1].wait_recv)
    transport(bins_mid, 1)
    lax.fori_loop(0, SUBSTEPS, collide, 0)
    for message in excesses[1]:
        message.wait_recv()
    finish(bins_out, 1)

    for it in range(ITERS):
        for has_to, has_from, message in halos[it]:
            when_do(has_to, message.wait_send)
        for message in excesses[it]:
            message.wait_send()
        when_do(x < gx - 1, faces[it].wait_send)
    for message in loads:
        message.wait_send()


def on_device(sizes, fields, courants, bin_moments, block_costs, block_owner, collision):
    nbin = collision.shape[0]
    courants = jnp.transpose(courants, (1, 0, 2))
    plan, extra, rows, main = pair_plan(nbin)
    wide = up(nbin * nbin, LANES)
    far = pl.BlockSpec(memory_space=pltpu.HBM)
    gx = sizes["gx"]
    cap, features, cells = bin_moments.shape
    width = fields.shape[1]
    places = 4 * gx
    padded = up(nbin, 8)
    vmem = pl.BlockSpec(memory_space=pltpu.VMEM)
    f32, bf16 = jnp.float32, jnp.bfloat16
    dma = pltpu.SemaphoreType.DMA
    return pl.pallas_call(
        functools.partial(coupled_kernel, sizes, nbin),
        out_shape=(
            jax.ShapeDtypeStruct(fields.shape, f32),
            jax.ShapeDtypeStruct(bin_moments.shape, bf16),
        ),
        in_specs=[far] * 6,
        out_specs=(vmem, vmem),
        scratch_shapes=[
            pltpu.SMEM(block_owner.shape, jnp.int32),
            pltpu.SMEM(block_costs.shape, jnp.int32),
            pltpu.SMEM((places,), jnp.int32),
            pltpu.SMEM((places,), jnp.int32),
            pltpu.SMEM((SUBSTEPS,), jnp.int32),
            pltpu.SMEM((cap,), jnp.int32),
            pltpu.VMEM(fields.shape, f32),
            pltpu.VMEM((16, cells), f32),
            pltpu.VMEM((gx, 16, cells), f32),
            pltpu.VMEM((ITERS, 8, cells), f32),
            pltpu.VMEM((gx, 8, cells), f32),
            pltpu.VMEM((gx, 8, cells), f32),
            pltpu.VMEM((ITERS, 2, width, LANES), f32),
            pltpu.VMEM((ITERS, 2, width, LANES), f32),
            pltpu.VMEM((ITERS, 2, width, cells), f32),
            pltpu.VMEM((ITERS, 2, width, cells), f32),
            pltpu.VMEM((ITERS, 4, width, cells), f32),
            pltpu.VMEM((ITERS, 4, width, cells), f32),
            pltpu.VMEM((ITERS, features, LANES), bf16),
            pltpu.VMEM((ITERS, features, LANES), bf16),
            pltpu.VMEM((2, 8, cells), f32),
            pltpu.VMEM(bin_moments.shape, bf16),
            pltpu.VMEM((cap, features, cells), f32),
            pltpu.VMEM((cap + SUBSTEPS, 2 * padded, cells), f32),
            pltpu.VMEM((padded, cells), f32),
            pltpu.VMEM((rows, cells), bf16),
            pltpu.VMEM(fields.shape, f32),
            pltpu.VMEM(courants.shape, f32),
            pltpu.VMEM(bin_moments.shape, bf16),
            pltpu.VMEM(collision.shape, bf16),
            pltpu.VMEM((LANES, wide), f32),
            pltpu.VMEM((wide, LANES), f32),
            pltpu.VMEM((rows, LANES), f32),
            pltpu.VMEM((up(nbin, 16), rows), bf16),
            dma((6,)),
            dma((gx - 1,)),
            dma((gx - 1,)),
            dma((ITERS, gx - 1)),
            dma((ITERS, gx - 1)),
            dma((ITERS, 8)),
            dma((ITERS, 8)),
            dma((ITERS,)),
            dma((ITERS,)),
        ],
        compiler_params=pltpu.CompilerParams(
            collective_id=0, has_side_effects=True, vmem_limit_bytes=60 * 1024 * 1024
        ),
    )(block_owner, block_costs, fields, courants, bin_moments, collision)


def solution(mesh):
    parts = P(("groups", "gx", "gy", "gz"), None, None)
    return jax.shard_map(
        functools.partial(on_device, dict(mesh.shape)),
        mesh=mesh,
        in_specs=(parts, parts, parts, P("groups"), P("groups"), P()),
        out_specs=(parts, parts),
        check_vma=False,
    )
```

```python
import functools
import math

import jax
import jax.numpy as jnp
from jax import lax
from jax.experimental import pallas as pl
from jax.experimental.pallas import tpu as pltpu
from jax.sharding import PartitionSpec as P

ITERS = 2
SUBSTEPS = 4
LATENT = 2.5
SAT_SCALE = 0.5
SAT_SLOPE = 0.2
GROWTH_RATE = 0.02
SOLUTE_WEIGHT = 0.5
LANES = 128
MESH = pl.DeviceIdType.MESH


def up(value, step):
    return -(-value // step) * step


def pair_plan(nbin):
    main = 8 * (nbin // 8)
    plan, extra, row = [], [], 0
    for i in range(main):
        low = 8 * (i // 8)
        plan.append((i, low, row))
        r = i - low
        if r >= 1:
            extra.append((row, i, main))
        if r >= 2:
            extra.append((row + 1, i, main + 1))
        if r == 6 and low == 0:
            extra += [(row + 2, main, main), (row + 3, main, main + 1), (row + 4, main + 1, main + 1)]
        if r == 7:
            extra += [(row + 2, low, main), (row + 3, low, main + 1), (row + 4, low + 1, main + 1)]
        row += main - low
    return plan, extra, row, main


def fold_kernel(nbin, c_ref, w_ref, by_pair, folded):
    plan, extra, rows, main = pair_plan(nbin)
    for start in range(0, c_ref.shape[1], LANES):
        by_pair[start : start + LANES, :] = c_ref[:, start : start + LANES].astype(jnp.float32).T
    for i, low, row in plan:
        length = main - low
        partner = low + lax.broadcasted_iota(jnp.int32, (length, LANES), 0)
        direct = by_pair[pl.ds(nbin * i + low, length), :]
        swapped = by_pair[pl.ds(nbin * low + i, length, stride=nbin), :]
        both = jnp.where(partner > i, direct + swapped, direct)
        folded[row : row + length, :] = jnp.where(partner >= i, both, 0.0)
    for row, i, j in extra:
        value = by_pair[nbin * i + j : nbin * i + j + 1, :]
        if i != j:
            value = value + by_pair[nbin * j + i : nbin * j + i + 1, :]
        folded[row : row + 1, :] = value
    for start in range(0, rows, LANES):
        chunk = folded[start : start + LANES, :].T
        w_ref[:, start : start + LANES] = chunk[: w_ref.shape[0]].astype(w_ref.dtype)


def fold(collision):
    nbin, pairs = collision.shape
    plan, extra, rows, main = pair_plan(nbin)
    depth = rows
    reach = up(max(pairs, nbin * (up(nbin, 8) - 1) + nbin), LANES)
    padded = jnp.pad(collision, ((0, LANES - nbin), (0, up(pairs, LANES) - pairs)))
    return pl.pallas_call(
        functools.partial(fold_kernel, nbin),
        out_shape=jax.ShapeDtypeStruct((up(nbin, 16), depth), jnp.bfloat16),
        in_specs=[pl.BlockSpec(memory_space=pltpu.VMEM)],
        out_specs=pl.BlockSpec(memory_space=pltpu.VMEM),
        scratch_shapes=[
            pltpu.VMEM((reach, LANES), jnp.float32),
            pltpu.VMEM((depth, LANES), jnp.float32),
        ],
        compiler_params=pltpu.CompilerParams(vmem_limit_bytes=32 * 1024 * 1024),
    )(padded)


def coupled_kernel(
    sizes, nbin,
    owner_ref, cost_ref, fields_ref, courants_ref, bins_ref, w_ref,
    fields_out, bins_out,
    owner_at, rank_at, cost_from, result_of,
    fields_mid, load_mine, load_all, excess_mine, excess_first, excess_second,
    x_low, x_high, y_low, y_high, z_low, z_high,
    face_mine, face_in, sums,
    bins_mid, moved, state, number, products,
    load_send, load_recv, excess_send, excess_recv, halo_send, halo_recv, face_send, face_recv,
):
    gx, gy, gz = sizes["gx"], sizes["gy"], sizes["gz"]
    x, y, z = lax.axis_index("gx"), lax.axis_index("gy"), lax.axis_index("gz")
    half = gx // 2
    places = 4 * gx
    cap = bins_ref.shape[0]
    cells = fields_ref.shape[2]
    columns = gy * gz
    column = y * gz + z
    last = cells - LANES
    f32 = jnp.float32
    padded = up(nbin, 8)
    excess_all = (excess_first, excess_second)

    barrier = pltpu.get_barrier_semaphore()
    for k in range(1, gx):
        pl.semaphore_signal(barrier, inc=1, device_id={"gx": lax.rem(x + k, gx)}, device_id_type=MESH)
    for name, index, count in (("gy", y, gy), ("gz", z, gz)):
        @pl.when(index > 0)
        def _():
            pl.semaphore_signal(barrier, inc=1, device_id={name: index - 1}, device_id_type=MESH)

        @pl.when(index < count - 1)
        def _():
            pl.semaphore_signal(barrier, inc=1, device_id={name: index + 1}, device_id_type=MESH)

    start = jnp.int32(0)
    count = jnp.int32(0)
    before = jnp.int32(-1)
    rank = jnp.int32(0)
    for p in range(places):
        block = (((p // 4 + half) % gx) * columns + column) * 4 + p % 4
        owner = owner_ref[block]
        rank = jnp.where(owner == before, rank + 1, 0)
        before = owner
        owner_at[p] = owner
        rank_at[p] = jnp.minimum(rank, cap - 1)
        start = start + jnp.where(owner < x, 1, 0)
        count = count + jnp.where(owner == x, 1, 0)
    first_row, valid = [], []
    ends = []
    total = jnp.int32(0)
    starts = []
    for s in range(cap):
        place = jnp.minimum(start + s, places - 1)
        tile = lax.rem(place // 4 + half, gx)
        block = (tile * columns + column) * 4 + lax.rem(place, 4)
        occupied = s < count
        valid.append(occupied)
        first_row.append((tile, lax.rem(place, 4)))
        steps = jnp.where(occupied, cost_ref[block], 0)
        starts.append(total)
        total = total + steps
        ends.append(total)
        result_of[s] = jnp.where(steps == 0, s, cap + jnp.clip(total - 1, 0, SUBSTEPS - 1))
    for t in range(SUBSTEPS):
        slot = jnp.int32(0)
        fresh = jnp.int32(0)
        for s in range(cap):
            slot = slot + jnp.where(ends[s] <= t, 1, 0)
            fresh = fresh + jnp.where((starts[s] == t) & (ends[s] > t), 1, 0)
        cost_from[t] = jnp.where(fresh > 0, jnp.minimum(slot, cap - 1), cap + t - 1)

    feature = lax.broadcasted_iota(jnp.int32, (8, bins_ref.shape[1]), 1)
    weights = jnp.where(
        feature >= 3 * nbin, 1.0, jnp.where(feature >= 2 * nbin, SOLUTE_WEIGHT, 0.0)
    ).astype(jnp.bfloat16)
    load_mine[...] = jnp.zeros(load_mine.shape, f32)
    for s in range(cap):
        summed = jnp.dot(weights, bins_ref[s], preferred_element_type=f32)
        load_mine[s : s + 1, :] = summed[0:1]
    for b in range(4):
        load_mine[8 + b : 9 + b, :] = courants_ref[b, 0:1, :]
    load_all[x] = load_mine[...]
    excess_mine[...] = jnp.zeros(excess_mine.shape, f32)

    near = lax.broadcasted_iota(jnp.int32, (1, LANES), 1) < LANES // 2

    def pack_face(ref, it):
        held = jnp.clip(count, 2, cap)
        upper = ref[held - 2, :, last:].astype(f32)
        lower = ref[held - 1, :, last:].astype(f32)
        packed = jnp.where(near, pltpu.roll(upper, LANES // 2, 1), lower)
        face_mine[it] = packed.astype(jnp.bfloat16)

    pack_face(bins_ref, 0)

    def copy(src, dst, send, recv, where):
        return pltpu.make_async_remote_copy(
            src_ref=src, dst_ref=dst, send_sem=send, recv_sem=recv,
            device_id=where, device_id_type=MESH,
        )

    def load_copies():
        return [
            copy(load_mine, load_all.at[x], load_send.at[k - 1], load_recv.at[k - 1],
                 {"gx": lax.rem(x + k, gx)})
            for k in range(1, gx)
        ]

    def excess_copies(it):
        return [
            copy(excess_mine.at[it], excess_all[it].at[x], excess_send.at[it, k - 1],
                 excess_recv.at[it, k - 1], {"gx": lax.rem(x + k, gx)})
            for k in range(1, gx)
        ]

    def halo_copies(src, it):
        out = []
        n = [0]

        def add(has_to, has_from, source, target, where):
            out.append((has_to, has_from, copy(
                source, target, halo_send.at[it, n[0]], halo_recv.at[it, n[0]], where)))
            n[0] += 1

        xu, xd = {"gx": lax.rem(x + 1, gx)}, {"gx": lax.rem(x + gx - 1, gx)}
        yu, yd = {"gy": lax.rem(y + 1, gy)}, {"gy": lax.rem(y + gy - 1, gy)}
        zu, zd = {"gz": lax.rem(z + 1, gz)}, {"gz": lax.rem(z + gz - 1, gz)}
        add(x < gx - 1, x > 0, src.at[pl.ds(2, 2), :, pl.ds(last, LANES)], x_low.at[it], xu)
        add(x > 0, x < gx - 1, src.at[pl.ds(0, 2), :, pl.ds(0, LANES)], x_high.at[it], xd)
        for a in range(2):
            add(y < gy - 1, y > 0, src.at[2 * a + 1], y_low.at[it, a], yu)
            add(y > 0, y < gy - 1, src.at[2 * a], y_high.at[it, a], yd)
        add(z < gz - 1, z > 0, src, z_low.at[it], zu)
        add(z > 0, z < gz - 1, src, z_high.at[it], zd)
        return out

    def face_copy(it):
        return copy(face_mine.at[it], face_in.at[it], face_send.at[it], face_recv.at[it],
                    {"gx": lax.rem(x + 1, gx)})

    def when_do(condition, action):
        @pl.when(condition)
        def _():
            action()

    for low, index in ((x_low, x), (y_low, y), (z_low, z)):
        def clear(low=low):
            low[...] = jnp.zeros(low.shape, f32)
        when_do(index == 0, clear)
    for high, index, size in ((x_high, x, gx), (y_high, y, gy), (z_high, z, gz)):
        def clear(high=high):
            high[...] = jnp.zeros(high.shape, f32)
        when_do(index == size - 1, clear)

    def clear_face():
        face_in[...] = jnp.zeros(face_in.shape, jnp.bfloat16)
    when_do(x == 0, clear_face)

    one = lambda flag: jnp.where(flag, 1, 0)
    pl.semaphore_wait(
        barrier, gx - 1 + one(y > 0) + one(y < gy - 1) + one(z > 0) + one(z < gz - 1)
    )

    halos = [halo_copies(fields_ref, 0), halo_copies(fields_mid, 1)]
    loads = load_copies()
    excesses = [excess_copies(it) for it in range(ITERS)]
    faces = [face_copy(it) for it in range(ITERS)]
    for has_to, has_from, message in halos[0]:
        when_do(has_to, message.start)
    for message in loads:
        message.start()
    when_do(x < gx - 1, faces[0].start)

    for message in loads:
        message.wait_recv()
    base = 4 * lax.rem(x + half, gx)
    sums[...] = jnp.zeros(sums.shape, f32)
    for q in range(6):
        place = jnp.maximum(base - 2 + q, 0)
        row = load_all[owner_at[place], pl.ds(rank_at[place], 1), :]
        if q < 2:
            row = jnp.where(base > 0, row, 0.0)
        sums[0, q : q + 1, :] = row
    sums[1, 0:2, :] = load_all[lax.rem(x + gx - 1, gx), 10:12, :]
    sums[1, 2:6, :] = load_mine[8:12, :]
    along = sums[1]
    cell = lax.broadcasted_iota(jnp.int32, (1, cells), 1)
    layer = LANES // 2

    def sum_transport(value):
        earlier = pltpu.roll(value, 2, 0)
        shifted = jnp.where(cell < layer, pltpu.roll(earlier, layer, 1), pltpu.roll(value, layer, 1))
        return value - along * (value - shifted)

    bin_sums = [sum_transport(sums[0])]
    bin_sums.append(sum_transport(bin_sums[0]))
    yc = lax.rem(cell // 8, 8)
    zc = lax.rem(cell, 8)
    kind = lax.broadcasted_iota(jnp.int32, (8, 1), 0)
    share = jnp.where(kind == 0, LATENT, jnp.where(kind == 1, -1.0, 0.0))

    def dynamics(src, dst, it):
        for has_to, has_from, message in halos[it]:
            when_do(has_from, message.wait_recv)
        for b in range(4):
            a, c = b // 2, b % 2
            g = src[b]
            west = src[b - 2, :, last:] if a else x_low[it, c]
            east = x_high[it, c] if a else src[b + 2, :, :LANES]
            south = src[b - 1] if c else y_low[it, a]
            north = y_high[it, a] if c else src[b + 1]
            wide = cells + LANES
            sides = (
                (pltpu.roll(jnp.concatenate([west, g], axis=1), layer, 1)[:, LANES:],
                 pltpu.roll(jnp.concatenate([g, east], axis=1), wide - layer, 1)[:, :cells]),
                (jnp.where(yc > 0, pltpu.roll(g, 8, 1), pltpu.roll(south, cells - 56, 1)),
                 jnp.where(yc < 7, pltpu.roll(g, cells - 8, 1), pltpu.roll(north, 56, 1))),
                (jnp.where(zc > 0, pltpu.roll(g, 1, 1), pltpu.roll(z_low[it, b], cells - 7, 1)),
                 jnp.where(zc < 7, pltpu.roll(g, cells - 1, 1), pltpu.roll(z_high[it, b], 7, 1))),
            )
            result = g
            for direction in range(3):
                low, high = sides[direction]
                component = courants_ref[b, direction : direction + 1, :]
                result = result - jnp.maximum(component, 0.0) * (g - low)
                result = result - jnp.minimum(component, 0.0) * (high - g)
            excess = result[1:2] - SAT_SCALE * jnp.exp(SAT_SLOPE * result[0:1])
            excess_mine[it, b : b + 1, :] = excess
            gained = GROWTH_RATE * excess * bin_sums[it][2 + b : 3 + b]
            dst[b] = result + share * gained
        excess_all[it][x] = excess_mine[it]
        for message in excesses[it]:
            message.start()

    bin_mass = jnp.exp(
        lax.broadcasted_iota(jnp.int32, (padded, 1), 0).astype(f32) * (math.log(8.0) / (nbin - 1))
    )
    plan, extra, rows, main = pair_plan(nbin)
    eighth = lax.broadcasted_iota(jnp.int32, (8, 1), 0)

    def transport(src, it):
        face = face_in[it].astype(f32)
        for s in range(cap):
            tile, row = first_row[s]
            courant = load_all[tile, pl.ds(8 + row, 1), :]
            if s == 0:
                left = face
            elif s == 1:
                left = pltpu.roll(face, layer, 1)
            else:
                left = pltpu.roll(src[s - 2, :, last:].astype(f32), layer, 1)
            for lane in range(0, cells, LANES):
                u = src[s, :, lane : lane + LANES].astype(f32)
                turned = pltpu.roll(u, layer, 1)
                shifted = jnp.where(near, left, turned)
                left = turned
                moved[s, :, lane : lane + LANES] = u - courant[:, lane : lane + LANES] * (u - shifted)
            state[s, :padded, :] = moved[s, :padded, :]
            state[s, padded:, :] = moved[s, nbin : nbin + padded, :]

    def collide(t, carried):
        source = cost_from[t]
        number[...] = state[source, :padded, :]
        above = number[main : main + 1, :]
        top = number[main + 1 : main + 2, :]
        above_first = jnp.where(eighth % 2 == 0, above, top)
        for m in range(0, main, 2):
            pieces = []
            for i, low, row in plan[m : m + 2]:
                r = i - low
                own = number[i : i + 1, :]
                diagonal = number[low : low + 8, :]
                left = own
                if r == 1:
                    diagonal = jnp.where(eighth == 0, above, diagonal)
                elif r >= 2:
                    diagonal = jnp.where(eighth < 2, above_first, diagonal)
                if r == 6 and low == 0:
                    left = jnp.where((eighth == 2) | (eighth == 3), above, own)
                    left = jnp.where(eighth == 4, top, left)
                if r == 7:
                    first, second = number[low : low + 1, :], number[low + 1 : low + 2, :]
                    left = jnp.where((eighth == 2) | (eighth == 3), first, own)
                    left = jnp.where(eighth == 4, second, left)
                if r == 7 or (r == 6 and low == 0):
                    middle = (eighth >= 2) & (eighth < 4)
                    diagonal = jnp.where(middle, above_first, diagonal)
                    diagonal = jnp.where(eighth == 4, top, diagonal)
                pieces.append(left * diagonal)
                if low + 8 < main:
                    pieces.append(own * number[low + 8 : main, :])
            pair = jnp.concatenate(pieces, axis=0)
            row = plan[m][2]
            products[row : row + pair.shape[0], :] = pair.astype(jnp.bfloat16)
        change = jnp.dot(w_ref[...], products[...], preferred_element_type=f32)[:padded]
        state[cap + t, :padded, :] = number[...] + change
        state[cap + t, padded:, :] = state[source, padded:, :] + bin_mass * change
        return carried

    def finish(dst, it):
        for s in range(cap):
            tile, row = first_row[s]
            excess = excess_all[it][tile, pl.ds(row, 1), :]
            final = result_of[s]
            growth = (GROWTH_RATE * excess) * (
                moved[s, 3 * nbin :, :] + SOLUTE_WEIGHT * moved[s, 2 * nbin : 3 * nbin, :]
            )
            moved[s, :nbin, :] = state[final, :nbin, :]
            moved[s, nbin : 2 * nbin, :] = state[final, padded : padded + nbin, :] + growth
            value = moved[s]
            if it == ITERS - 1:
                value = jnp.where(valid[s], value, 0.0)
            dst[s] = value.astype(jnp.bfloat16)

    dynamics(fields_ref, fields_mid, 0)
    for has_to, has_from, message in halos[1]:
        when_do(has_to, message.start)
    when_do(x > 0, faces[0].wait_recv)
    transport(bins_ref, 0)
    lax.fori_loop(0, SUBSTEPS, collide, 0)
    for message in excesses[0]:
        message.wait_recv()
    finish(bins_mid, 0)
    pack_face(bins_mid, 1)
    when_do(x < gx - 1, faces[1].start)
    dynamics(fields_mid, fields_out, 1)
    when_do(x > 0, faces[1].wait_recv)
    transport(bins_mid, 1)
    lax.fori_loop(0, SUBSTEPS, collide, 0)
    for message in excesses[1]:
        message.wait_recv()
    finish(bins_out, 1)

    for it in range(ITERS):
        for has_to, has_from, message in halos[it]:
            when_do(has_to, message.wait_send)
        for message in excesses[it]:
            message.wait_send()
        when_do(x < gx - 1, faces[it].wait_send)
    for message in loads:
        message.wait_send()


def on_device(sizes, fields, courants, bin_moments, block_costs, block_owner, collision):
    nbin = collision.shape[0]
    folded = fold(collision)
    gx = sizes["gx"]
    cap, features, cells = bin_moments.shape
    width = fields.shape[1]
    places = 4 * gx
    padded = up(nbin, 8)
    vmem = pl.BlockSpec(memory_space=pltpu.VMEM)
    smem = pl.BlockSpec(memory_space=pltpu.SMEM)
    f32, bf16 = jnp.float32, jnp.bfloat16
    dma = pltpu.SemaphoreType.DMA
    return pl.pallas_call(
        functools.partial(coupled_kernel, sizes, nbin),
        out_shape=(
            jax.ShapeDtypeStruct(fields.shape, f32),
            jax.ShapeDtypeStruct(bin_moments.shape, bf16),
        ),
        in_specs=[smem, smem, vmem, vmem, vmem, vmem],
        out_specs=(vmem, vmem),
        scratch_shapes=[
            pltpu.SMEM((places,), jnp.int32),
            pltpu.SMEM((places,), jnp.int32),
            pltpu.SMEM((SUBSTEPS,), jnp.int32),
            pltpu.SMEM((cap,), jnp.int32),
            pltpu.VMEM(fields.shape, f32),
            pltpu.VMEM((16, cells), f32),
            pltpu.VMEM((gx, 16, cells), f32),
            pltpu.VMEM((ITERS, 8, cells), f32),
            pltpu.VMEM((gx, 8, cells), f32),
            pltpu.VMEM((gx, 8, cells), f32),
            pltpu.VMEM((ITERS, 2, width, LANES), f32),
            pltpu.VMEM((ITERS, 2, width, LANES), f32),
            pltpu.VMEM((ITERS, 2, width, cells), f32),
            pltpu.VMEM((ITERS, 2, width, cells), f32),
            pltpu.VMEM((ITERS, 4, width, cells), f32),
            pltpu.VMEM((ITERS, 4, width, cells), f32),
            pltpu.VMEM((ITERS, features, LANES), bf16),
            pltpu.VMEM((ITERS, features, LANES), bf16),
            pltpu.VMEM((2, 8, cells), f32),
            pltpu.VMEM(bin_moments.shape, bf16),
            pltpu.VMEM((cap, features, cells), f32),
            pltpu.VMEM((cap + SUBSTEPS, 2 * padded, cells), f32),
            pltpu.VMEM((padded, cells), f32),
            pltpu.VMEM((folded.shape[1], cells), bf16),
            dma((gx - 1,)),
            dma((gx - 1,)),
            dma((ITERS, gx - 1)),
            dma((ITERS, gx - 1)),
            dma((ITERS, 8)),
            dma((ITERS, 8)),
            dma((ITERS,)),
            dma((ITERS,)),
        ],
        compiler_params=pltpu.CompilerParams(
            collective_id=0, has_side_effects=True, vmem_limit_bytes=48 * 1024 * 1024
        ),
    )(block_owner, block_costs, fields, courants, bin_moments, folded)


def solution(mesh):
    parts = P(("groups", "gx", "gy", "gz"), None, None)
    return jax.shard_map(
        functools.partial(on_device, dict(mesh.shape)),
        mesh=mesh,
        in_specs=(parts, parts, parts, P("groups"), P("groups"), P()),
        out_specs=(parts, parts),
        check_vma=False,
    )
```
